128 devices in a mesh: lon: 32 (over z_lo, x, y), lat: 4 (over z_hi, core).
Axes of the slice: x: 4, y: 4, z: 4 (z_hi: 2, z_lo: 2; z = z_hi * 2 + z_lo), core: 2. Of those that a mesh axis runs over, the one named last changes fastest.
Arguments:
- initial_state: float32 [3, 3072, 4096], P(None, 'lat', 'lon'), may hold values from -6 to 6
- bottom_drag: float32 [3072, 4096], P('lat', 'lon'), may hold values from 0.05 to 1
- drag_direction: float32 [3072, 4096], P('lat', 'lon'), may hold values from -5 to 5
- land_mask: int32 [3072, 4096], P('lat', 'lon'), may hold values 0 or 1
- section_cells: int32 [8192], replicated, may hold values from 0 to 12582911
- section_sign: int32 [8192], replicated, may hold values from -1 to 1
Outputs:
- curvature: float32 [3072, 4096], P('lat', 'lon')
- final_state: float32 [3, 3072, 4096], P(None, 'lat', 'lon')
- final_tangent: float32 [3, 3072, 4096], P(None, 'lat', 'lon')
The draws below stay inside these ranges and needn't reach their ends.
All inputs are finite; a program needn't handle non-finite values. No bound on the sum of `land_mask` on one device may be relied on, other than what follows from the above.
Results may differ from the reference program's by a relative error of at most 0.00002.
Values sent between devices are 32-bit elements; how exact they have to be, the bound alone decides.
A program may use at most 128 MiB of HBM per device.

```python
import math
import jax
import jax.numpy as jnp

ITERS = 6
NX = 4096
NY = 3072
SECT = 8192


def touch_ends(values, stream_key, least, high):
    index_at = [jax.random.randint(jax.random.fold_in(stream_key, axis), (), 0, length) for axis, length in enumerate(values.shape)]
    main_axis = values.shape.index(max(values.shape))
    beside = index_at[:main_axis] + [(index_at[main_axis] + 1) % values.shape[main_axis]] + index_at[main_axis + 1:]
    return values.at[tuple(index_at)].set(least).at[tuple(beside)].set(high)


def block_scale(rng, dims, shards, low, largest):
    gain = 1.0
    for dim, blocks in shards:
        steps = jax.random.uniform(jax.random.fold_in(jax.random.fold_in(rng, 6), dim), (blocks,), jnp.float32, low / len(shards), largest / len(shards))
        gain = gain * jnp.repeat(jnp.exp(steps), dims[dim] // blocks).reshape((-1,) + (1,) * (len(dims) - 1 - dim))
    return gain


def noise(stream_key, dims, deviation, limit, pieces=(), held_as=jnp.bfloat16):
    level = block_scale(stream_key, dims, pieces, -0.22, 0.18) if pieces else 1.0
    result = jax.random.normal(stream_key, dims, jnp.float32) * deviation * level
    return jnp.minimum(jnp.maximum(result, -limit), limit).astype(held_as)


def setup_inputs(seed: int = 0) -> dict:
    arg_keys = jax.random.split(jax.random.key(seed), 7)
    initial_state = noise(arg_keys[0], (3, NY, NX), 1.0, 6.0, ((1, 4), (2, 32)), jnp.float32)
    bottom_drag = jnp.clip(jnp.exp(math.log(1.0) - 2.9957323 * jax.random.uniform(arg_keys[1], (NY, NX), jnp.float32) ** block_scale(arg_keys[1], (NY, NX), ((0, 4), (1, 32)), -0.2, 0.2)), 0.05, 1.0)
    drag_direction = noise(arg_keys[2], (NY, NX), 1.0, 5.0, ((0, 4), (1, 32)), jnp.float32)
    land_mask = touch_ends((jax.random.randint(arg_keys[3], (NY, NX), 0, 8) < 7).astype(jnp.int32), jax.random.fold_in(arg_keys[3], 1), 0, 1)
    section_cells = touch_ends(jax.random.randint(arg_keys[4], (SECT,), 0, NY * NX), jax.random.fold_in(arg_keys[4], 1), 0, (NY * NX) - 1).astype(jnp.int32)
    section_sign = touch_ends(jax.random.randint(arg_keys[5], (SECT,), -1, 2), jax.random.fold_in(arg_keys[5], 1), -1, 1).astype(jnp.int32)
    return dict(initial_state=initial_state, bottom_drag=bottom_drag, drag_direction=drag_direction, land_mask=land_mask, section_cells=section_cells, section_sign=section_sign)


wave_step = 0.4
coriolis = 0.25

def across(field):
    return 0.5 * (field[1:-1, 2:] - field[1:-1, :-2])

def along(field):
    return 0.5 * (field[2:, 1:-1] - field[:-2, 1:-1])

def advance(padded, drag_field, ocean):
    height = padded[0]
    zonal = padded[1]
    meridional = padded[2]
    height_mid = height[1:-1, 1:-1]
    zonal_mid = zonal[1:-1, 1:-1]
    merid_mid = meridional[1:-1, 1:-1]
    damping = ocean / (1.0 + drag_field)
    new_height = (height_mid - wave_step * (across(zonal) + along(meridional))) * ocean
    new_zonal = (zonal_mid - wave_step * across(height) + coriolis * merid_mid) * damping
    new_merid = (merid_mid - wave_step * along(height) - coriolis * zonal_mid) * damping
    return jnp.stack([new_height, new_zonal, new_merid])

def pad_global(fields, signs):
    count = fields.shape[0]
    columns = jnp.concatenate([fields[:, :, -1:], fields, fields[:, :, :1]], axis=2)
    folded = fields[:, -1, ::-1] * signs[:, None]
    corner = jnp.zeros((count, 1, 1), fields.dtype)
    south = jnp.concatenate([corner, jnp.zeros((count, 1, fields.shape[2]), fields.dtype), corner], axis=2)
    north = jnp.concatenate([corner, folded[:, None, :], corner], axis=2)
    return jnp.concatenate([south, columns, north], axis=1)

def reference(initial_state, bottom_drag, drag_direction, land_mask, section_cells, section_sign):
    ocean = land_mask.astype(jnp.float32)
    signs = jnp.array([1.0, -1.0, -1.0], jnp.float32)
    weights = jnp.zeros((NY * NX,), jnp.float32).at[section_cells].add(section_sign.astype(jnp.float32)).reshape(NY, NX)

    def integrate(drag_field):
        state = initial_state * ocean[None]
        for unused in range(ITERS):
            state = advance(pad_global(state, signs), drag_field, ocean)
        return state

    def transport(drag_field):
        return jnp.sum(weights * integrate(drag_field)[2])
    curvature = jax.jvp(jax.grad(transport), (bottom_drag,), (drag_direction,))[1]
    final_state, final_tangent = jax.jvp(integrate, (bottom_drag,), (drag_direction,))
    return (curvature, final_state, final_tangent)
```

```python
import functools

import jax
import jax.numpy as jnp
from jax import lax
from jax.experimental import pallas as pl
from jax.experimental.pallas import tpu as pltpu
from jax.sharding import PartitionSpec as P

ITERS = 6
SLABS = 7
PAD = 8
MESH = pl.DeviceIdType.MESH


def exchange_kernel(
    init_ref, drag_ref, dir_ref, mask_ref, cells_ref, sign_ref,
    t_ref, w_ref,
    nat, flip, acc, fold_acc, send_sem, recv_sem,
):
    rows, cols = drag_ref.shape
    ext = cols + 2 * PAD
    n_lon, n_lat = lax.axis_size("lon"), lax.axis_size("lat")
    lon, lat = lax.axis_index("lon"), lax.axis_index("lat")
    top = lat == n_lat - 1
    east, west = lax.rem(lon + 1, n_lon), lax.rem(lon + n_lon - 1, n_lon)

    def device(lon_at, lat_at):
        return {"lon": lon_at, "lat": lat_at}

    barrier = pltpu.get_barrier_semaphore()

    def greet(target):
        pl.semaphore_signal(barrier, inc=1, device_id=target, device_id_type=MESH)

    greet(device(east, lat))
    greet(device(west, lat))

    @pl.when(top)
    def _():
        greet(device(n_lon - 1 - lon, lat))

    @pl.when(jnp.logical_not(top))
    def _():
        greet(device(lon, lat + 1))

    @pl.when(lat > 0)
    def _():
        greet(device(lon, lat - 1))

    def prepare(part, carry):
        here = pl.ds(pl.multiple_of(part * 64, 64), 64)
        there = pl.ds(pl.multiple_of(part * 64 + PAD, 8), 64)
        ocean = mask_ref[here, :].astype(jnp.float32)
        inverse = 1.0 / (1.0 + drag_ref[here, :])
        nat[0, there, :] = init_ref[0, here, :] * (0.2 * ocean)
        nat[1, there, :] = init_ref[1, here, :] * ocean
        nat[2, there, :] = init_ref[2, here, :] * ocean
        nat[3, there, :] = ocean * inverse
        nat[4, there, :] = -(dir_ref[here, :] * inverse)
        return carry

    lax.fori_loop(0, rows // 64, prepare, 0)
    tail = rows + 2 * PAD
    for f in range(5):
        nat[f, tail:, :] = jnp.zeros((nat.shape[1] - tail, cols), jnp.float32)

    lanes = lax.broadcasted_iota(jnp.int32, (PAD, cols), 1)
    for f in range(5):
        tile = nat[f, rows : rows + PAD, :]
        turned = jnp.take_along_axis(tile, cols - 1 - lanes, axis=1)
        if f in (1, 2):
            turned = -turned
        for k in range(PAD):
            flip[f, k : k + 1, :] = turned[PAD - 1 - k : PAD - k, :]

    south_halo, north_halo = pl.ds(0, PAD), pl.ds(rows + PAD, PAD)

    def copy(src, dst, which, slot, target):
        return pltpu.make_async_remote_copy(
            src_ref=src, dst_ref=dst, send_sem=send_sem.at[which],
            recv_sem=recv_sem.at[slot], device_id=target, device_id_type=MESH,
        )

    fold_copy = copy(flip, nat.at[:, north_halo, :], 0, 1, device(n_lon - 1 - lon, lat))
    north_copy = copy(
        nat.at[:, pl.ds(rows, PAD), :], nat.at[:, south_halo, :], 0, 0, device(lon, lat + 1)
    )
    south_copy = copy(
        nat.at[:, pl.ds(PAD, PAD), :], nat.at[:, north_halo, :], 1, 1, device(lon, lat - 1)
    )
    east_copy = copy(
        t_ref.at[:, :, pl.ds(cols, PAD), :], t_ref.at[:, :, pl.ds(0, PAD), :],
        2, 2, device(east, lat),
    )
    west_copy = copy(
        t_ref.at[:, :, pl.ds(PAD, PAD), :], t_ref.at[:, :, pl.ds(cols + PAD, PAD), :],
        3, 3, device(west, lat),
    )

    pl.semaphore_wait(barrier, jnp.where(lat > 0, 4, 3))

    @pl.when(top)
    def _():
        fold_copy.start()

    @pl.when(jnp.logical_not(top))
    def _():
        north_copy.start()

    @pl.when(lat > 0)
    def _():
        south_copy.start()

    @pl.when(lat == 0)
    def _():
        for f in range(5):
            nat[f, 0:PAD, :] = jnp.zeros((PAD, cols), jnp.float32)

    total = cols * n_lon
    chunk = cells_ref.shape[1]
    low = (SLABS + 1) // 2
    a_iota = lax.broadcasted_iota(jnp.int32, (2 * ext, chunk), 0)
    b_iota = lax.broadcasted_iota(jnp.int32, (low * 128, chunk), 0)
    f_iota = lax.broadcasted_iota(jnp.int32, (16, chunk), 0)
    contract = (((1,), (1,)), ((), ()))
    acc[...] = jnp.zeros_like(acc)
    fold_acc[...] = jnp.zeros_like(fold_acc)

    def gather_weights(part, carry):
        cell = cells_ref[pl.ds(part, 1), :]
        sign = sign_ref[pl.ds(part, 1), :].astype(jnp.float32)
        row, col = lax.div(cell, total), lax.rem(cell, total)
        r = row - lat * rows + PAD
        lane = lax.shift_right_arithmetic(r * 9363, 16)
        slab = r - lane * SLABS
        c = col - lon * cols + PAD
        c = jnp.where(c < 0, c + total, c)
        c = jnp.where(c >= total, c - total, c)
        in_rows = (r >= 0) & (r < rows + 2 * PAD)
        a_at = jnp.where(c < ext, (slab // low) * ext + c, -1)
        b_at = jnp.where(in_rows, (slab % low) * 128 + lane, -1)
        a = jnp.where(a_iota == a_at, 1.0, 0.0).astype(jnp.bfloat16)
        b = jnp.where(b_iota == b_at, sign, 0.0).astype(jnp.bfloat16)
        acc[...] += lax.dot_general(a, b, contract, preferred_element_type=jnp.float32)
        fr = 2 * rows - 1 - (row - lat * rows) - rows
        fr = jnp.where(top, fr, -1)
        fc = total - 1 - col - lon * cols + PAD
        fc = jnp.where(fc < 0, fc + total, fc)
        fc = jnp.where(fc >= total, fc - total, fc)
        fa = jnp.where(a_iota[:ext] == fc, 1.0, 0.0).astype(jnp.bfloat16)
        fb = jnp.where((f_iota == fr) & (f_iota < PAD), -sign, 0.0).astype(jnp.bfloat16)
        fold_acc[:, 0:16] += lax.dot_general(
            fa, fb, contract, preferred_element_type=jnp.float32
        )
        return carry

    parts = cells_ref.shape[0]
    lax.fori_loop(0, parts // 2, gather_weights, 0)

    @pl.when(lat > 0)
    def _():
        north_copy.wait_recv()

    south_copy.wait_recv()

    for f in range(5):
        for j in range(SLABS):
            t_ref[f, j, PAD : cols + PAD, :] = nat[f, pl.ds(j, 128, stride=SLABS), :].T
    east_copy.start()
    west_copy.start()

    lax.fori_loop(parts // 2, parts, gather_weights, 0)
    column = lax.broadcasted_iota(jnp.int32, (ext, 128), 1)
    ghosts = fold_acc[...]
    for j in range(SLABS):
        hi, lo = divmod(j, low)
        found = acc[hi * ext : (hi + 1) * ext, lo * 128 : (lo + 1) * 128]
        for k in range(PAD):
            lane, slab = divmod(rows + PAD + k, SLABS)
            if slab == j:
                found += jnp.where(column == lane, pltpu.roll(ghosts, lane - k, 1), 0.0)
        w_ref[j] = found

    east_copy.wait_recv()
    west_copy.wait_recv()
    east_copy.wait_send()
    west_copy.wait_send()
    north_copy.wait_send()

    @pl.when(lat > 0)
    def _():
        south_copy.wait_send()


def chain_kernel(
    t_ref, w_ref, curv_ref, state_ref, tangent_ref, levels, back, curv, nat
):
    cols = t_ref.shape[2] - 2 * PAD
    rows = curv_ref.shape[0]
    tiles = t_ref.shape[2] // 8

    def rows_at(i, shift=0):
        return pl.ds(PAD + 8 * i + shift, 8)

    def step(src, dst, i, spin):
        here = pl.ds(8 * i, 8)
        damp = [t_ref[3, j, here, :] for j in range(SLABS)]
        factor = [t_ref[4, j, here, :] for j in range(SLABS)]
        scale = [jnp.where(d > 0.0, 0.04, 0.0) for d in damp]
        new = [[], []]
        for part in range(2):
            h, u, v = 3 * part, 3 * part + 1, 3 * part + 2
            hs = [src[h, j, rows_at(i), :] for j in range(SLABS)]
            vs = [src[v, j, rows_at(i), :] for j in range(SLABS)]
            h_up, h_down = pltpu.roll(hs[0], 127, 1), pltpu.roll(hs[-1], 1, 1)
            v_up, v_down = pltpu.roll(vs[0], 127, 1), pltpu.roll(vs[-1], 1, 1)
            for j in range(SLABS):
                north_h = hs[j + 1] if j < SLABS - 1 else h_up
                south_h = hs[j - 1] if j > 0 else h_down
                north_v = vs[j + 1] if j < SLABS - 1 else v_up
                south_v = vs[j - 1] if j > 0 else v_down
                um = src[u, j, rows_at(i), :]
                du = src[u, j, rows_at(i, 1), :] - src[u, j, rows_at(i, -1), :]
                dh = src[h, j, rows_at(i, 1), :] - src[h, j, rows_at(i, -1), :]
                new_h = hs[j] - scale[j] * (du + (north_v - south_v))
                new_u = (um - dh + spin * vs[j]) * damp[j]
                new_v = (vs[j] - (north_h - south_h) - spin * um) * damp[j]
                if part == 1:
                    new_u += factor[j] * new[0][j][0]
                    new_v += factor[j] * new[0][j][1]
                dst[h, j, rows_at(i), :] = new_h
                dst[u, j, rows_at(i), :] = new_u
                dst[v, j, rows_at(i), :] = new_v
                new[part].append((new_u, new_v))
        return new

    zero = jnp.zeros((8, 128), jnp.float32)
    for field in range(6):
        for j in range(SLABS):
            for n in range(ITERS + 1):
                levels[n, field, j, 0:PAD, :] = zero
                levels[n, field, j, cols + 3 * PAD :, :] = zero
            for n in range(2):
                back[n, field, j, 0:PAD, :] = zero
                back[n, field, j, cols + 3 * PAD :, :] = zero

    def start(i, carry):
        for j in range(SLABS):
            for field in range(3):
                levels[0, field, j, rows_at(i), :] = t_ref[field, j, pl.ds(8 * i, 8), :]
                levels[0, 3 + field, j, rows_at(i), :] = zero
            weight = t_ref[3, j, pl.ds(8 * i, 8), :] * w_ref[j, pl.ds(8 * i, 8), :]
            for field in (0, 1, 3, 4):
                back[0, field, j, rows_at(i), :] = zero
            back[0, 2, j, rows_at(i), :] = weight
            back[0, 5, j, rows_at(i), :] = weight * t_ref[4, j, pl.ds(8 * i, 8), :]
        return carry

    lax.fori_loop(0, tiles, start, 0)

    def forward(n, carry):
        for i in range(tiles):
            step(levels.at[n], levels.at[n + 1], i, 0.25)
        return carry

    lax.fori_loop(0, ITERS, forward, 0)

    for out, first in ((state_ref, 0), (tangent_ref, 3)):
        for field in range(3):
            for j in range(SLABS):
                block = levels[ITERS, first + field, j, 2 * PAD : 2 * PAD + cols, :].T
                if field == 0:
                    block = block * 5.0
                nat[first + field, pl.ds(j, 128, stride=SLABS), :] = block
            out[field] = nat[first + field, PAD : PAD + rows, :]

    for i in range(1, tiles - 1):
        for j in range(SLABS):
            at = rows_at(i)
            curv[j, pl.ds(8 * i - 8, 8), :] = -(
                levels[ITERS, 5, j, at, :] * back[0, 2, j, at, :]
                + levels[ITERS, 2, j, at, :] * back[0, 5, j, at, :]
            )

    def backward(k, carry):
        src, dst = back.at[lax.rem(k, 2)], back.at[lax.rem(k + 1, 2)]
        level = levels.at[ITERS - 1 - k]
        for i in range(tiles):
            new = step(src, dst, i, -0.25)
            if 0 < i < tiles - 1:
                for j in range(SLABS):
                    at, own = rows_at(i), pl.ds(8 * i - 8, 8)
                    (qu, qv), (ru, rv) = new[0][j], new[1][j]
                    curv[j, own, :] -= (
                        levels_uv(level, 4, j, at) * qu + levels_uv(level, 5, j, at) * qv
                    ) + (levels_uv(level, 1, j, at) * ru + levels_uv(level, 2, j, at) * rv)
        return carry

    def levels_uv(level, field, j, at):
        return level[field, j, at, :]

    lax.fori_loop(0, ITERS - 1, backward, 0)
    for j in range(SLABS):
        nat[6, pl.ds(j, 128, stride=SLABS), :] = curv[j].T
    curv_ref[...] = nat[6, PAD : PAD + rows, :]


def on_device(initial_state, bottom_drag, drag_direction, land_mask, section_cells, section_sign):
    rows, cols = bottom_drag.shape
    ext = cols + 2 * PAD
    f32 = jnp.float32
    vmem = pl.BlockSpec(memory_space=pltpu.VMEM)
    chunk = 512
    fields, weights = pl.pallas_call(
        exchange_kernel,
        out_shape=(
            jax.ShapeDtypeStruct((5, SLABS, ext, 128), f32),
            jax.ShapeDtypeStruct((SLABS, ext, 128), f32),
        ),
        in_specs=[vmem] * 6,
        out_specs=(vmem, vmem),
        scratch_shapes=[
            pltpu.VMEM((5, SLABS * 128, cols), f32),
            pltpu.VMEM((5, PAD, cols), f32),
            pltpu.VMEM((2 * ext, (SLABS + 1) // 2 * 128), f32),
            pltpu.VMEM((ext, 128), f32),
            pltpu.SemaphoreType.DMA((4,)),
            pltpu.SemaphoreType.DMA((4,)),
        ],
        compiler_params=pltpu.CompilerParams(
            collective_id=0, has_side_effects=True, vmem_limit_bytes=40 * 1024 * 1024
        ),
        name="exchange",
    )(
        initial_state, bottom_drag, drag_direction, land_mask,
        section_cells.reshape(-1, chunk), section_sign.reshape(-1, chunk),
    )
    return pl.pallas_call(
        chain_kernel,
        out_shape=(
            jax.ShapeDtypeStruct((rows, cols), f32),
            jax.ShapeDtypeStruct((3, rows, cols), f32),
            jax.ShapeDtypeStruct((3, rows, cols), f32),
        ),
        in_specs=[vmem] * 2,
        out_specs=(vmem, vmem, vmem),
        scratch_shapes=[
            pltpu.VMEM((ITERS + 1, 6, SLABS, ext + 2 * PAD, 128), f32),
            pltpu.VMEM((2, 6, SLABS, ext + 2 * PAD, 128), f32),
            pltpu.VMEM((SLABS, cols, 128), f32),
            pltpu.VMEM((7, SLABS * 128, cols), f32),
        ],
        compiler_params=pltpu.CompilerParams(vmem_limit_bytes=56 * 1024 * 1024),
        name="chain",
    )(fields, weights)


def solution(mesh):
    return jax.shard_map(
        on_device,
        mesh=mesh,
        in_specs=(
            P(None, "lat", "lon"),
            P("lat", "lon"),
            P("lat", "lon"),
            P("lat", "lon"),
            P(),
            P(),
        ),
        out_specs=(P("lat", "lon"), P(None, "lat", "lon"), P(None, "lat", "lon")),
        check_vma=False,
    )
```

```python
import functools

import jax
import jax.numpy as jnp
from jax import lax
from jax.experimental import pallas as pl
from jax.experimental.pallas import tpu as pltpu
from jax.sharding import PartitionSpec as P

ITERS = 6
SLABS = 7
LOW = (SLABS + 1) // 2
PAD = 8
CHUNK = 8
MESH = pl.DeviceIdType.MESH


def exchange_kernel(
    init_hbm, drag_hbm, dir_hbm, mask_hbm, cells_hbm, sign_hbm,
    t_hbm, w_hbm,
    t_ref, w_ref, init_ref, drag_ref, dir_ref, mask_ref, cells_ref, sign_ref,
    nat, flip, at_ref, acc, fold_acc, load_sem, send_sem, recv_sem, out_sem,
):
    rows, cols = drag_ref.shape
    ext = cols + 2 * PAD
    n_lon, n_lat = lax.axis_size("lon"), lax.axis_size("lat")
    lon, lat = lax.axis_index("lon"), lax.axis_index("lat")
    top = lat == n_lat - 1
    east, west = lax.rem(lon + 1, n_lon), lax.rem(lon + n_lon - 1, n_lon)

    loads = [
        pltpu.make_async_copy(src, dst, load_sem.at[k])
        for k, (src, dst) in enumerate((
            (mask_hbm, mask_ref), (drag_hbm, drag_ref), (init_hbm, init_ref),
            (dir_hbm, dir_ref), (cells_hbm, cells_ref), (sign_hbm, sign_ref),
        ))
    ]
    for load in loads:
        load.start()

    def device(lon_at, lat_at):
        return {"lon": lon_at, "lat": lat_at}

    barrier = pltpu.get_barrier_semaphore()

    def greet(target):
        pl.semaphore_signal(barrier, inc=1, device_id=target, device_id_type=MESH)

    greet(device(east, lat))
    greet(device(west, lat))

    @pl.when(top)
    def _():
        greet(device(n_lon - 1 - lon, lat))

    @pl.when(jnp.logical_not(top))
    def _():
        greet(device(lon, lat + 1))

    @pl.when(lat > 0)
    def _():
        greet(device(lon, lat - 1))

    def prepare(part, carry):
        here = pl.ds(pl.multiple_of(part * 64, 64), 64)
        there = pl.ds(pl.multiple_of(part * 64 + PAD, 8), 64)
        ocean = mask_ref[here, :].astype(jnp.float32)
        inverse = 1.0 / (1.0 + drag_ref[here, :])
        nat[0, there, :] = init_ref[0, here, :] * (0.2 * ocean)
        nat[1, there, :] = init_ref[1, here, :] * ocean
        nat[2, there, :] = init_ref[2, here, :] * ocean
        nat[3, there, :] = ocean * inverse
        nat[4, there, :] = -(dir_ref[here, :] * inverse)
        return carry

    tail = rows + 2 * PAD
    for f in range(5):
        nat[f, tail:, :] = jnp.zeros((nat.shape[1] - tail, cols), jnp.float32)
    for load in loads:
        load.wait()
    lax.fori_loop(0, rows // 64, prepare, 0)

    lanes = lax.broadcasted_iota(jnp.int32, (PAD, cols), 1)
    for f in range(5):
        tile = nat[f, rows : rows + PAD, :]
        turned = jnp.take_along_axis(tile, cols - 1 - lanes, axis=1)
        if f in (1, 2):
            turned = -turned
        for k in range(PAD):
            flip[f, k : k + 1, :] = turned[PAD - 1 - k : PAD - k, :]

    south_halo, north_halo = pl.ds(0, PAD), pl.ds(rows + PAD, PAD)

    def copy(src, dst, which, slot, target):
        return pltpu.make_async_remote_copy(
            src_ref=src, dst_ref=dst, send_sem=send_sem.at[which],
            recv_sem=recv_sem.at[slot], device_id=target, device_id_type=MESH,
        )

    fold_copy = copy(flip, nat.at[:, north_halo, :], 0, 1, device(n_lon - 1 - lon, lat))
    north_copy = copy(
        nat.at[:, pl.ds(rows, PAD), :], nat.at[:, south_halo, :], 0, 0, device(lon, lat + 1)
    )
    south_copy = copy(
        nat.at[:, pl.ds(PAD, PAD), :], nat.at[:, north_halo, :], 1, 1, device(lon, lat - 1)
    )
    east_copy = copy(
        t_ref.at[:, :, pl.ds(cols, PAD), :], t_ref.at[:, :, pl.ds(0, PAD), :],
        2, 2, device(east, lat),
    )
    west_copy = copy(
        t_ref.at[:, :, pl.ds(PAD, PAD), :], t_ref.at[:, :, pl.ds(cols + PAD, PAD), :],
        3, 3, device(west, lat),
    )

    pl.semaphore_wait(barrier, jnp.where(lat > 0, 4, 3))

    @pl.when(top)
    def _():
        fold_copy.start()

    @pl.when(jnp.logical_not(top))
    def _():
        north_copy.start()

    @pl.when(lat > 0)
    def _():
        south_copy.start()

    @pl.when(lat == 0)
    def _():
        for f in range(5):
            nat[f, 0:PAD, :] = jnp.zeros((PAD, cols), jnp.float32)

    total = cols * n_lon
    cell = cells_ref[...]
    row, col = lax.div(cell, total), lax.rem(cell, total)
    r = row - lat * rows + PAD
    lane = lax.shift_right_arithmetic(r * 9363, 16)
    slab = r - lane * SLABS
    c = col - lon * cols + PAD
    c = jnp.where(c < 0, c + total, c)
    c = jnp.where(c >= total, c - total, c)
    in_rows = (r >= 0) & (r < rows + 2 * PAD)
    at_ref[0] = jnp.where(c < ext, lax.div(slab, LOW) * ext + c, -1)
    at_ref[1] = jnp.where(in_rows, lax.rem(slab, LOW) * 128 + lane, -1)
    fr = rows - 1 - (row - lat * rows)
    at_ref[2] = jnp.where(top & (fr < PAD), fr, -1)
    fc = total - 1 - col - lon * cols + PAD
    fc = jnp.where(fc < 0, fc + total, fc)
    at_ref[3] = jnp.where(fc >= total, fc - total, fc)

    contract = (((1,), (1,)), ((), ()))
    acc[...] = jnp.zeros_like(acc)
    fold_acc[...] = jnp.zeros_like(fold_acc)

    def spread(which, at):
        line = at_ref[which, pl.ds(at, 1), :]
        return jnp.broadcast_to(line, (16, 128)).astype(jnp.int16)

    def one_hot(which, first, size, value=None):
        steps = lax.broadcasted_iota(jnp.int16, (size, 128), 0)
        found = []
        for k in range(CHUNK):
            at = jnp.concatenate([spread(which, first + k)] * (size // 16), axis=0)
            if value is None:
                hit = jnp.ones((size, 128), jnp.bfloat16)
            else:
                hit = jnp.concatenate([value[k]] * (size // 16), axis=0)
            found.append(jnp.where(steps == at, hit, jnp.zeros((size, 128), jnp.bfloat16)))
        return jnp.concatenate(found, axis=1)

    def gather_weights(part, carry):
        first = part * CHUNK
        signs = [
            jnp.broadcast_to(sign_ref[pl.ds(first + k, 1), :], (16, 128))
            .astype(jnp.float32).astype(jnp.bfloat16)
            for k in range(CHUNK)
        ]
        a = one_hot(0, first, 2 * ext)
        b = one_hot(1, first, LOW * 128, signs)
        acc[...] += lax.dot_general(a, b, contract, preferred_element_type=jnp.float32)
        fa = one_hot(3, first, ext)
        fb = one_hot(2, first, 16, signs)
        fold_acc[:, 0:16] += lax.dot_general(
            fa, fb, contract, preferred_element_type=jnp.float32
        )
        return carry

    parts = cells_ref.shape[0] // CHUNK
    lax.fori_loop(0, parts // 2, gather_weights, 0)

    @pl.when(lat > 0)
    def _():
        north_copy.wait_recv()

    south_copy.wait_recv()

    for f in range(5):
        for j in range(SLABS):
            t_ref[f, j, PAD : cols + PAD, :] = nat[f, pl.ds(j, 128, stride=SLABS), :].T
    east_copy.start()
    west_copy.start()

    def store(start, size, which):
        part = pl.ds(start, size)
        return pltpu.make_async_copy(
            t_ref.at[:, :, part, :], t_hbm.at[:, :, part, :], out_sem.at[which]
        )

    own_out = store(PAD, cols, 0)
    own_out.start()

    lax.fori_loop(parts // 2, parts, gather_weights, 0)
    column = lax.broadcasted_iota(jnp.int32, (ext, 128), 1)
    ghosts = fold_acc[...]
    for j in range(SLABS):
        hi, lo = divmod(j, LOW)
        found = acc[hi * ext : (hi + 1) * ext, lo * 128 : (lo + 1) * 128]
        for k in range(PAD):
            lane_at, slab_at = divmod(rows + PAD + k, SLABS)
            if slab_at == j:
                turned = pltpu.roll(ghosts, lane_at - k, 1)
                found -= jnp.where(column == lane_at, turned, 0.0)
        w_ref[j] = found
    w_out = pltpu.make_async_copy(w_ref, w_hbm, out_sem.at[1])
    w_out.start()

    east_copy.wait_recv()
    east_out = store(0, PAD, 2)
    east_out.start()
    west_copy.wait_recv()
    west_out = store(cols + PAD, PAD, 3)
    west_out.start()
    east_copy.wait_send()
    west_copy.wait_send()
    north_copy.wait_send()

    @pl.when(lat > 0)
    def _():
        south_copy.wait_send()

    own_out.wait()
    w_out.wait()
    east_out.wait()
    west_out.wait()


def chain_kernel(
    t_hbm, w_hbm, curv_hbm, state_hbm, tangent_hbm,
    t_ref, w_ref, levels, back_a, back_b, scale_ref, curv, nat, load_sem, out_sem,
):
    ext = t_ref.shape[2]
    cols = ext - 2 * PAD
    rows = curv_hbm.shape[0]
    tiles = ext // 8
    third = ext // 3

    loads = [
        pltpu.make_async_copy(
            t_hbm.at[:, :, pl.ds(k * third, third), :],
            t_ref.at[:, :, pl.ds(k * third, third), :], load_sem.at[k],
        )
        for k in range(3)
    ] + [pltpu.make_async_copy(w_hbm, w_ref, load_sem.at[3])]
    for load in loads:
        load.start()

    def around(src, field, j, i):
        if i == 0:
            low = pltpu.roll(src[field, j, 0:8, :], 1, 0)
        else:
            low = src[field, j, 8 * i - 1 : 8 * i + 7, :]
        if i == tiles - 1:
            high = pltpu.roll(src[field, j, 8 * i : 8 * i + 8, :], 7, 0)
        else:
            high = src[field, j, 8 * i + 1 : 8 * i + 9, :]
        return high - low

    def step(src, dst, i, spin, use=None, first=False):
        here = slice(8 * i, 8 * i + 8)
        parts = (0,) if first else (0, 3)

        def get(field, j):
            return src[field, j, here, :]

        up = {f: pltpu.roll(get(f, 0), 127, 1) for p in parts for f in (p, p + 2)}
        before = {f: pltpu.roll(get(f, SLABS - 1), 1, 1) for p in parts for f in (p, p + 2)}
        now = {f: get(f, 0) for p in parts for f in (p, p + 2)}
        for j in range(SLABS):
            damp, factor = t_ref[3, j, here, :], t_ref[4, j, here, :]
            if first:
                scale = jnp.where(damp > 0.0, 0.04, 0.0)
                scale_ref[j, here, :] = scale
            else:
                scale = scale_ref[j, here, :]
            after = {
                f: get(f, j + 1) if j < SLABS - 1 else up[f] for p in parts for f in (p, p + 2)
            }
            new = []
            for p in parts:
                h, u, v = p, p + 1, p + 2
                um, vm = get(u, j), now[v]
                new_h = now[h] - scale * (around(src, u, j, i) + (after[v] - before[v]))
                new_u = (um - around(src, h, j, i) + spin * vm) * damp
                new_v = (vm - (after[h] - before[h]) - spin * um) * damp
                if p:
                    new_u += factor * new[0]
                    new_v += factor * new[1]
                new += [new_u, new_v]
                dst[h, j, here, :] = new_h
                dst[u, j, here, :] = new_u
                dst[v, j, here, :] = new_v
            if first:
                new += [factor * new[0], factor * new[1]]
                dst[3, j, here, :] = jnp.zeros((8, 128), jnp.float32)
                dst[4, j, here, :] = new[2]
                dst[5, j, here, :] = new[3]
            if use is not None:
                use(j, i, here, new)
            before, now = now, after

    def weigh(level):
        def use(j, i, here, new):
            if 0 < i < tiles - 1:
                qu, qv, ru, rv = new
                own = slice(8 * i - 8, 8 * i)
                curv[j, own, :] -= (
                    level[4, j, here, :] * qu + level[5, j, here, :] * qv
                ) + (level[1, j, here, :] * ru + level[2, j, here, :] * rv)
        return use

    def turn(field, times=None):
        for j in range(SLABS):
            block = levels[ITERS - 1, field, j, PAD : PAD + cols, :]
            if times is not None:
                block = block * times
            nat[field, pl.ds(j, 128, stride=SLABS), :] = block.T

    def send(field, out, at):
        return pltpu.make_async_copy(
            nat.at[field, pl.ds(PAD, rows), :], out.at[at], out_sem.at[field]
        )

    ready = 0
    for i in range(tiles):
        while ready < 3 and ready * third < 8 * i + 9:
            loads[ready].wait()
            ready += 1
        step(t_ref, levels.at[0], i, 0.25, first=True)

    def forward(n, carry):
        for i in range(tiles):
            step(levels.at[n], levels.at[n + 1], i, 0.25)
        return carry

    lax.fori_loop(0, ITERS - 1, forward, 0)

    loads[3].wait()
    last, prior = levels.at[ITERS - 1], levels.at[ITERS - 2]
    for i in range(tiles):
        here = slice(8 * i, 8 * i + 8)
        q = [t_ref[3, j, here, :] * w_ref[j, here, :] for j in range(SLABS)]
        r = [t_ref[4, j, here, :] * q[j] for j in range(SLABS)]
        q = [pltpu.roll(q[-1], 1, 1)] + q + [pltpu.roll(q[0], 127, 1)]
        r = [pltpu.roll(r[-1], 1, 1)] + r + [pltpu.roll(r[0], 127, 1)]
        for j in range(SLABS):
            damp, factor = t_ref[3, j, here, :], t_ref[4, j, here, :]
            scale = scale_ref[j, here, :]
            qv, rv = q[j + 1] * damp, r[j + 1] * damp
            qu, ru = -0.25 * qv, -0.25 * rv
            rv, ru = rv + factor * qv, ru + factor * qu
            back_a[0, j, here, :] = scale * (q[j] - q[j + 2])
            back_a[1, j, here, :] = qu
            back_a[2, j, here, :] = qv
            back_a[3, j, here, :] = scale * (r[j] - r[j + 2])
            back_a[4, j, here, :] = ru
            back_a[5, j, here, :] = rv
            if 0 < i < tiles - 1:
                done = last[5, j, here, :] * q[j + 1] + last[2, j, here, :] * r[j + 1]
                done += prior[4, j, here, :] * qu + prior[5, j, here, :] * qv
                done += prior[1, j, here, :] * ru + prior[2, j, here, :] * rv
                curv[j, 8 * i - 8 : 8 * i, :] = -done
    turn(0, 5.0)
    turn(3, 5.0)
    send(0, state_hbm, 0).start()
    send(3, tangent_hbm, 0).start()

    def backward(k, carry):
        turn(1 + k)
        for i in range(tiles):
            step(back_a, back_b, i, -0.25, weigh(levels.at[ITERS - 3 - 2 * k]))
        send(1 + k, state_hbm, 1 + k).start()
        turn(4 + k)
        for i in range(tiles):
            step(back_b, back_a, i, -0.25, weigh(levels.at[ITERS - 4 - 2 * k]))
        send(4 + k, tangent_hbm, 1 + k).start()
        return carry

    lax.fori_loop(0, (ITERS - 2) // 2, backward, 0)
    for j in range(SLABS):
        nat[6, pl.ds(j, 128, stride=SLABS), :] = curv[j].T
    curv_copy = pltpu.make_async_copy(nat.at[6, pl.ds(PAD, rows), :], curv_hbm, out_sem.at[6])
    curv_copy.start()
    for f in range(3):
        send(f, state_hbm, f).wait()
        send(3 + f, tangent_hbm, f).wait()
    curv_copy.wait()


def on_device(initial_state, bottom_drag, drag_direction, land_mask, section_cells, section_sign):
    rows, cols = bottom_drag.shape
    ext = cols + 2 * PAD
    f32, i32 = jnp.float32, jnp.int32
    hbm = pl.BlockSpec(memory_space=pl.ANY)
    lines = section_cells.shape[0] // 128
    fields, weights = pl.pallas_call(
        exchange_kernel,
        out_shape=(
            jax.ShapeDtypeStruct((5, SLABS, ext, 128), f32),
            jax.ShapeDtypeStruct((SLABS, ext, 128), f32),
        ),
        in_specs=[hbm] * 6,
        out_specs=(hbm, hbm),
        scratch_shapes=[
            pltpu.VMEM((5, SLABS, ext, 128), f32),
            pltpu.VMEM((SLABS, ext, 128), f32),
            pltpu.VMEM((3, rows, cols), f32),
            pltpu.VMEM((rows, cols), f32),
            pltpu.VMEM((rows, cols), f32),
            pltpu.VMEM((rows, cols), i32),
            pltpu.VMEM((lines, 128), i32),
            pltpu.VMEM((lines, 128), i32),
            pltpu.VMEM((5, SLABS * 128, cols), f32),
            pltpu.VMEM((5, PAD, cols), f32),
            pltpu.VMEM((4, lines, 128), i32),
            pltpu.VMEM((2 * ext, LOW * 128), f32),
            pltpu.VMEM((ext, 128), f32),
            pltpu.SemaphoreType.DMA((6,)),
            pltpu.SemaphoreType.DMA((4,)),
            pltpu.SemaphoreType.DMA((4,)),
            pltpu.SemaphoreType.DMA((4,)),
        ],
        compiler_params=pltpu.CompilerParams(
            collective_id=0, has_side_effects=True, vmem_limit_bytes=56 * 1024 * 1024
        ),
        name="exchange",
    )(
        initial_state, bottom_drag, drag_direction, land_mask,
        section_cells.reshape(lines, 128), section_sign.reshape(lines, 128),
    )
    return pl.pallas_call(
        chain_kernel,
        out_shape=(
            jax.ShapeDtypeStruct((rows, cols), f32),
            jax.ShapeDtypeStruct((3, rows, cols), f32),
            jax.ShapeDtypeStruct((3, rows, cols), f32),
        ),
        in_specs=[hbm] * 2,
        out_specs=(hbm, hbm, hbm),
        scratch_shapes=[
            pltpu.VMEM((5, SLABS, ext, 128), f32),
            pltpu.VMEM((SLABS, ext, 128), f32),
            pltpu.VMEM((ITERS, 6, SLABS, ext, 128), f32),
            pltpu.VMEM((6, SLABS, ext, 128), f32),
            pltpu.VMEM((6, SLABS, ext, 128), f32),
            pltpu.VMEM((SLABS, ext, 128), f32),
            pltpu.VMEM((SLABS, cols, 128), f32),
            pltpu.VMEM((7, SLABS * 128, cols), f32),
            pltpu.SemaphoreType.DMA((4,)),
            pltpu.SemaphoreType.DMA((7,)),
        ],
        compiler_params=pltpu.CompilerParams(vmem_limit_bytes=56 * 1024 * 1024),
        name="chain",
    )(fields, weights)


def solution(mesh):
    return jax.shard_map(
        on_device,
        mesh=mesh,
        in_specs=(
            P(None, "lat", "lon"),
            P("lat", "lon"),
            P("lat", "lon"),
            P("lat", "lon"),
            P(),
            P(),
        ),
        out_specs=(P("lat", "lon"), P(None, "lat", "lon"), P(None, "lat", "lon")),
        check_vma=False,
    )
```

```python
import functools

import jax
import jax.numpy as jnp
from jax import lax
from jax.experimental import pallas as pl
from jax.experimental.pallas import tpu as pltpu
from jax.sharding import PartitionSpec as P

ITERS = 6
SLABS = 7
LOW = (SLABS + 1) // 2
PAD = 8
HALO_LANES = (17, 24, 49, 56, 81)
CHUNK = 8
MESH = pl.DeviceIdType.MESH


def patched(tile, halo_rows, f, j):
    lane = lax.broadcasted_iota(jnp.int32, tile.shape, 1)
    rolled = pltpu.roll(halo_rows, (128 - HALO_LANES[f] - j) % 128, 1)
    north = 111 if j < 4 else 110
    here = lane == 0 if j == 4 else (lane == 0) | (lane == north)
    return jnp.where(here, rolled, tile)


def exchange_kernel(
    init_hbm, drag_hbm, dir_hbm, mask_hbm, cells_hbm, sign_hbm,
    t_hbm, patch_hbm, w_hbm,
    t_ref, w_ref, init_ref, drag_ref, dir_ref, mask_ref, cells_ref, sign_ref,
    nat, edge, strip, from_west, from_east, north_tile, halo, pack, patch, side,
    at_ref, acc, fold_acc, load_sem, send_sem, recv_sem, out_sem,
):
    rows, cols = drag_ref.shape
    ext = cols + 2 * PAD
    n_lon, n_lat = lax.axis_size("lon"), lax.axis_size("lat")
    lon, lat = lax.axis_index("lon"), lax.axis_index("lat")
    top = lat == n_lat - 1
    inner = lat > 0

    loads = [
        pltpu.make_async_copy(src, dst, load_sem.at[k])
        for k, (src, dst) in enumerate((
            (mask_hbm, mask_ref), (drag_hbm, drag_ref), (init_hbm, init_ref),
            (dir_hbm, dir_ref), (cells_hbm, cells_ref), (sign_hbm, sign_ref),
        ))
    ]
    for load in loads:
        load.start()

    def around(at, by):
        return lax.rem(at + by + n_lon, n_lon)

    up_lat = jnp.where(top, lat, lat + 1)
    up_lon = jnp.where(top, n_lon - 1 - lon, lon)
    up_slot = jnp.where(top, 3, 0)
    turns = (0, 1, -1)
    ups = [around(up_lon, by) for by in turns]
    downs = [around(lon, by) for by in turns]
    own_fold = [top & (at == lon) for at in ups]

    def device(lon_at, lat_at):
        return {"lon": lon_at, "lat": lat_at}

    barrier = pltpu.get_barrier_semaphore()

    def greet(lon_at, lat_at):
        pl.semaphore_signal(
            barrier, inc=1, device_id=device(lon_at, lat_at), device_id_type=MESH
        )

    greet(around(lon, 1), lat)
    greet(around(lon, -1), lat)
    peers = 2
    for k in range(3):
        pl.when(jnp.logical_not(own_fold[k]))(functools.partial(greet, ups[k], up_lat))
        pl.when(inner)(functools.partial(greet, downs[k], lat - 1))
        peers += jnp.where(own_fold[k], 0, 1) + jnp.where(inner, 1, 0)

    lane_of = lax.broadcasted_iota(jnp.int32, (64, cols), 1)

    def prepare(part, carry):
        here = pl.ds(pl.multiple_of(part * 64, 64), 64)
        there = pl.ds(pl.multiple_of(part * 64 + PAD, 8), 64)
        ocean = mask_ref[here, :].astype(jnp.float32)
        inverse = 1.0 / (1.0 + drag_ref[here, :])
        fields = [
            init_ref[0, here, :] * (0.2 * ocean),
            init_ref[1, here, :] * ocean,
            init_ref[2, here, :] * ocean,
            ocean * inverse,
            -(dir_ref[here, :] * inverse),
        ]
        sides = pltpu.roll(fields[0], 8, 1)
        for f in range(5):
            nat[f, there, :] = fields[f]
            if f:
                sides = jnp.where(
                    lane_of < 16 * f, sides, pltpu.roll(fields[f], 16 * f + 8, 1)
                )
        edge[there, :] = sides
        return carry

    height = nat.shape[1]
    tail = rows + PAD
    for f in range(5):
        nat[f, 0:PAD, :] = jnp.zeros((PAD, cols), jnp.float32)
        nat[f, tail:, :] = jnp.zeros((height - tail, cols), jnp.float32)
    edge[0:PAD, :] = jnp.zeros((PAD, cols), jnp.float32)
    edge[tail:, :] = jnp.zeros((height - tail, cols), jnp.float32)
    for load in loads:
        load.wait()
    lax.fori_loop(0, rows // 64, prepare, 0)

    @pl.when(jnp.logical_not(top))
    def _():
        north_tile[...] = nat[:, rows : rows + PAD, :]

    @pl.when(top)
    def _():
        lanes = lax.broadcasted_iota(jnp.int32, (PAD, cols), 1)
        for f in range(5):
            tile = nat[f, rows : rows + PAD, :]
            turned = jnp.take_along_axis(tile, cols - 1 - lanes, axis=1)
            if f in (1, 2):
                turned = -turned
            for k in range(PAD):
                north_tile[f, k : k + 1, :] = turned[PAD - 1 - k : PAD - k, :]

    @pl.when(lat == 0)
    def _():
        for k in range(3):
            halo[k] = jnp.zeros((5, PAD, cols), jnp.float32)

    for k in range(1, 3):
        @pl.when(own_fold[k])
        def _():
            halo[3 + k] = north_tile[...]

    def copy(src, dst, which, slot, lon_at, lat_at):
        return pltpu.make_async_remote_copy(
            src_ref=src, dst_ref=dst, send_sem=send_sem.at[which],
            recv_sem=recv_sem.at[slot], device_id=device(lon_at, lat_at),
            device_id_type=MESH,
        )

    up_copies = [
        copy(north_tile, halo.at[up_slot + k], k, up_slot + k, ups[k], up_lat)
        for k in range(3)
    ]
    down_copies = [
        copy(nat.at[:, pl.ds(PAD, PAD), :], halo.at[3 + k], 3 + k, 3 + k, downs[k], lat - 1)
        for k in range(3)
    ]
    east_copy = copy(
        strip.at[:, pl.ds(0, 5), pl.ds(0, 8), :], from_west, 6, 6, around(lon, 1), lat
    )
    west_copy = copy(
        strip.at[:, pl.ds(0, 5), pl.ds(8, 8), :], from_east, 7, 7, around(lon, -1), lat
    )

    pl.semaphore_wait(barrier, peers)
    for k in range(3):
        pl.when(jnp.logical_not(own_fold[k]))(up_copies[k].start)
        pl.when(inner)(down_copies[k].start)
    for j in range(SLABS):
        turned = edge[pl.ds(j + 1, 128, stride=SLABS), :].T
        for f in range(5):
            strip[j, f] = turned[16 * f : 16 * f + 16]
    east_copy.start()
    west_copy.start()

    for f in range(5):
        for j in range(SLABS):
            t_ref[f, j, PAD : cols + PAD, :] = nat[f, pl.ds(j + 1, 128, stride=SLABS), :].T

    def store(start, size, which):
        part = pl.ds(start, size)
        return pltpu.make_async_copy(
            t_ref.at[:, :, part, :], t_hbm.at[:, :, part, :], out_sem.at[which]
        )

    own_out = store(PAD, cols, 0)
    own_out.start()

    total = cols * n_lon
    cell = cells_ref[...]
    row, col = lax.div(cell, total), lax.rem(cell, total)
    r = row - lat * rows + SLABS
    lane = lax.shift_right_arithmetic(r * 9363, 16)
    slab = r - lane * SLABS
    c = col - lon * cols + PAD
    c = jnp.where(c < 0, c + total, c)
    c = jnp.where(c >= total, c - total, c)
    in_rows = (r >= 0) & (r < rows + 2 * SLABS)
    at_ref[0] = jnp.where(c < ext, lax.div(slab, LOW) * ext + c, -1)
    at_ref[1] = jnp.where(in_rows, lax.rem(slab, LOW) * 128 + lane, -1)
    fr = rows - 1 - (row - lat * rows)
    at_ref[2] = jnp.where(top & (fr < SLABS), fr, -1)
    fc = total - 1 - col - lon * cols + PAD
    fc = jnp.where(fc < 0, fc + total, fc)
    at_ref[3] = jnp.where(fc >= total, fc - total, fc)

    contract = (((1,), (1,)), ((), ()))
    acc[...] = jnp.zeros_like(acc)
    fold_acc[...] = jnp.zeros_like(fold_acc)

    def spread(which, at):
        line = at_ref[which, pl.ds(at, 1), :]
        return jnp.broadcast_to(line, (16, 128)).astype(jnp.int16)

    def one_hot(which, first, size, value=None):
        steps = lax.broadcasted_iota(jnp.int16, (size, 128), 0)
        found = []
        for k in range(CHUNK):
            at = jnp.concatenate([spread(which, first + k)] * (size // 16), axis=0)
            if value is None:
                hit = jnp.ones((size, 128), jnp.bfloat16)
            else:
                hit = jnp.concatenate([value[k]] * (size // 16), axis=0)
            found.append(jnp.where(steps == at, hit, jnp.zeros((size, 128), jnp.bfloat16)))
        return jnp.concatenate(found, axis=1)

    def gather_weights(part, carry):
        first = part * CHUNK
        signs = [
            jnp.broadcast_to(sign_ref[pl.ds(first + k, 1), :], (16, 128))
            .astype(jnp.float32).astype(jnp.bfloat16)
            for k in range(CHUNK)
        ]
        a = one_hot(0, first, 2 * ext)
        b = one_hot(1, first, LOW * 128, signs)
        acc[...] += lax.dot_general(a, b, contract, preferred_element_type=jnp.float32)
        fa = one_hot(3, first, ext)
        fb = one_hot(2, first, 16, signs)
        fold_acc[:, 0:16] += lax.dot_general(
            fa, fb, contract, preferred_element_type=jnp.float32
        )
        return carry

    lax.fori_loop(0, cells_ref.shape[0] // CHUNK, gather_weights, 0)
    column = lax.broadcasted_iota(jnp.int32, (ext, 128), 1)
    ghosts = fold_acc[...]
    for j in range(SLABS):
        hi, lo = divmod(j, LOW)
        found = acc[hi * ext : (hi + 1) * ext, lo * 128 : (lo + 1) * 128]
        for k in range(SLABS):
            lane_at, slab_at = divmod(rows + SLABS + k, SLABS)
            if slab_at == j:
                turned = pltpu.roll(ghosts, lane_at - k, 1)
                found -= jnp.where(column == lane_at, turned, 0.0)
        w_ref[j] = found
    w_out = pltpu.make_async_copy(w_ref, w_hbm, out_sem.at[1])
    w_out.start()

    for k in range(3):
        pl.when(inner)(
            copy(north_tile, halo.at[k], k, k, ups[k], up_lat).wait_recv
        )
        pl.when(jnp.logical_not(own_fold[k]))(
            copy(north_tile, halo.at[3 + k], k, 3 + k, ups[k], up_lat).wait_recv
        )
    pack[...] = jnp.zeros_like(pack)
    for k in range(3):
        for f in range(5):
            at = HALO_LANES[f]
            pack[k, at : at + 7, :] = halo[k, f, 1:8, :]
            pack[k, at - 17 : at - 13, :] = halo[3 + k, f, 2:6, :]
            pack[k, at - 13 : at - 11, :] = halo[3 + k, f, 0:2, :]
    patch[...] = pack[0].T
    patch_out = pltpu.make_async_copy(patch, patch_hbm, out_sem.at[2])
    patch_out.start()
    side[0] = pack[1].T[cols - PAD : cols]
    side[1] = pack[2].T[0:PAD]
    for k, got, sent, place in ((0, from_west, east_copy, 0), (1, from_east, west_copy, cols + PAD)):
        sent.wait_recv()
        for f in range(5):
            for j in range(SLABS):
                t_ref[f, j, place : place + PAD, :] = patched(got[j, f], side[k], f, j)
    west_out = store(0, PAD, 3)
    west_out.start()
    east_out = store(cols + PAD, PAD, 4)
    east_out.start()

    east_copy.wait_send()
    west_copy.wait_send()
    for k in range(3):
        pl.when(jnp.logical_not(own_fold[k]))(up_copies[k].wait_send)
        pl.when(inner)(down_copies[k].wait_send)
    own_out.wait()
    w_out.wait()
    patch_out.wait()
    west_out.wait()
    east_out.wait()


def chain_kernel(
    t_hbm, patch_hbm, w_hbm, curv_hbm, state_hbm, tangent_hbm,
    t_ref, patch_ref, w_ref, levels, back_a, back_b, scale_ref, curv, nat, load_sem, out_sem,
):
    ext = t_ref.shape[2]
    cols = ext - 2 * PAD
    rows = curv_hbm.shape[0]
    tiles = ext // 8
    third = ext // 3

    patch_load = pltpu.make_async_copy(patch_hbm, patch_ref, load_sem.at[4])
    patch_load.start()
    loads = [
        pltpu.make_async_copy(
            t_hbm.at[:, :, pl.ds(k * third, third), :],
            t_ref.at[:, :, pl.ds(k * third, third), :], load_sem.at[k],
        )
        for k in range(3)
    ] + [pltpu.make_async_copy(w_hbm, w_ref, load_sem.at[3])]
    for load in loads:
        load.start()

    def around(src, field, j, i):
        if i == 0:
            low = pltpu.roll(src[field, j, 0:8, :], 1, 0)
        else:
            low = src[field, j, 8 * i - 1 : 8 * i + 7, :]
        if i == tiles - 1:
            high = pltpu.roll(src[field, j, 8 * i : 8 * i + 8, :], 7, 0)
        else:
            high = src[field, j, 8 * i + 1 : 8 * i + 9, :]
        return high - low

    def step(src, dst, i, spin, use=None, first=False):
        here = slice(8 * i, 8 * i + 8)
        parts = (0,) if first else (0, 3)

        def get(field, j):
            return src[field, j, here, :]

        up = {f: pltpu.roll(get(f, 0), 127, 1) for p in parts for f in (p, p + 2)}
        before = {f: pltpu.roll(get(f, SLABS - 1), 1, 1) for p in parts for f in (p, p + 2)}
        now = {f: get(f, 0) for p in parts for f in (p, p + 2)}
        for j in range(SLABS):
            damp, factor = t_ref[3, j, here, :], t_ref[4, j, here, :]
            if first:
                scale = jnp.where(damp > 0.0, 0.04, 0.0)
                scale_ref[j, here, :] = scale
            else:
                scale = scale_ref[j, here, :]
            after = {
                f: get(f, j + 1) if j < SLABS - 1 else up[f] for p in parts for f in (p, p + 2)
            }
            new = []
            for p in parts:
                h, u, v = p, p + 1, p + 2
                um, vm = get(u, j), now[v]
                new_h = now[h] - scale * (around(src, u, j, i) + (after[v] - before[v]))
                new_u = (um - around(src, h, j, i) + spin * vm) * damp
                new_v = (vm - (after[h] - before[h]) - spin * um) * damp
                if p:
                    new_u += factor * new[0]
                    new_v += factor * new[1]
                new += [new_u, new_v]
                dst[h, j, here, :] = new_h
                dst[u, j, here, :] = new_u
                dst[v, j, here, :] = new_v
            if first:
                new += [factor * new[0], factor * new[1]]
                dst[3, j, here, :] = jnp.zeros((8, 128), jnp.float32)
                dst[4, j, here, :] = new[2]
                dst[5, j, here, :] = new[3]
            if use is not None:
                use(j, i, here, new)
            before, now = now, after

    def weigh(level):
        def use(j, i, here, new):
            if 0 < i < tiles - 1:
                qu, qv, ru, rv = new
                own = slice(8 * i - 8, 8 * i)
                curv[j, own, :] -= (
                    level[4, j, here, :] * qu + level[5, j, here, :] * qv
                ) + (level[1, j, here, :] * ru + level[2, j, here, :] * rv)
        return use

    def turn(field, times=None):
        for j in range(SLABS):
            block = levels[ITERS - 1, field, j, PAD : PAD + cols, :]
            if times is not None:
                block = block * times
            nat[field, pl.ds(j + 1, 128, stride=SLABS), :] = block.T

    def send(field, out, at):
        return pltpu.make_async_copy(
            nat.at[field, pl.ds(PAD, rows), :], out.at[at], out_sem.at[field]
        )

    patch_load.wait()
    for i in range(tiles + 1):
        if i % (tiles // 3) == 0 and i < tiles:
            loads[i // (tiles // 3)].wait()
        if 0 < i < tiles - 1:
            here = slice(8 * i, 8 * i + 8)
            halo_rows = patch_ref[8 * i - PAD : 8 * i - PAD + 8, :]
            for f in range(5):
                for j in range(SLABS):
                    t_ref[f, j, here, :] = patched(t_ref[f, j, here, :], halo_rows, f, j)
        if i == 0:
            continue
        i -= 1
        step(t_ref, levels.at[0], i, 0.25, first=True)

    def forward(n, carry):
        for i in range(tiles):
            step(levels.at[n], levels.at[n + 1], i, 0.25)
        return carry

    lax.fori_loop(0, ITERS - 1, forward, 0)

    loads[3].wait()
    last, prior = levels.at[ITERS - 1], levels.at[ITERS - 2]
    for i in range(tiles):
        here = slice(8 * i, 8 * i + 8)
        q = [t_ref[3, j, here, :] * w_ref[j, here, :] for j in range(SLABS)]
        r = [t_ref[4, j, here, :] * q[j] for j in range(SLABS)]
        q = [pltpu.roll(q[-1], 1, 1)] + q + [pltpu.roll(q[0], 127, 1)]
        r = [pltpu.roll(r[-1], 1, 1)] + r + [pltpu.roll(r[0], 127, 1)]
        for j in range(SLABS):
            damp, factor = t_ref[3, j, here, :], t_ref[4, j, here, :]
            scale = scale_ref[j, here, :]
            qv, rv = q[j + 1] * damp, r[j + 1] * damp
            qu, ru = -0.25 * qv, -0.25 * rv
            rv, ru = rv + factor * qv, ru + factor * qu
            back_a[0, j, here, :] = scale * (q[j] - q[j + 2])
            back_a[1, j, here, :] = qu
            back_a[2, j, here, :] = qv
            back_a[3, j, here, :] = scale * (r[j] - r[j + 2])
            back_a[4, j, here, :] = ru
            back_a[5, j, here, :] = rv
            if 0 < i < tiles - 1:
                done = last[5, j, here, :] * q[j + 1] + last[2, j, here, :] * r[j + 1]
                done += prior[4, j, here, :] * qu + prior[5, j, here, :] * qv
                done += prior[1, j, here, :] * ru + prior[2, j, here, :] * rv
                curv[j, 8 * i - 8 : 8 * i, :] = -done
    turn(0, 5.0)
    turn(3, 5.0)
    send(0, state_hbm, 0).start()
    send(3, tangent_hbm, 0).start()

    def backward(k, carry):
        turn(1 + k)
        for i in range(tiles):
            step(back_a, back_b, i, -0.25, weigh(levels.at[ITERS - 3 - 2 * k]))
        send(1 + k, state_hbm, 1 + k).start()
        turn(4 + k)
        for i in range(tiles):
            step(back_b, back_a, i, -0.25, weigh(levels.at[ITERS - 4 - 2 * k]))
        send(4 + k, tangent_hbm, 1 + k).start()
        return carry

    lax.fori_loop(0, (ITERS - 2) // 2, backward, 0)
    for j in range(SLABS):
        nat[6, pl.ds(j + 1, 128, stride=SLABS), :] = curv[j].T
    curv_copy = pltpu.make_async_copy(nat.at[6, pl.ds(PAD, rows), :], curv_hbm, out_sem.at[6])
    curv_copy.start()
    for f in range(3):
        send(f, state_hbm, f).wait()
        send(3 + f, tangent_hbm, f).wait()
    curv_copy.wait()


def on_device(initial_state, bottom_drag, drag_direction, land_mask, section_cells, section_sign):
    rows, cols = bottom_drag.shape
    ext = cols + 2 * PAD
    f32, i32 = jnp.float32, jnp.int32
    hbm = pl.BlockSpec(memory_space=pl.ANY)
    lines = section_cells.shape[0] // 128
    tall = SLABS * 128 + 8
    vm, dma = pltpu.VMEM, pltpu.SemaphoreType.DMA
    fields = jax.ShapeDtypeStruct((5, SLABS, ext, 128), f32)
    weights = jax.ShapeDtypeStruct((SLABS, ext, 128), f32)
    patches = jax.ShapeDtypeStruct((cols, 128), f32)
    fields, patches, weights = pl.pallas_call(
        exchange_kernel,
        out_shape=(fields, patches, weights),
        in_specs=[hbm] * 6,
        out_specs=(hbm, hbm, hbm),
        scratch_shapes=[
            vm(fields.shape, f32),
            vm(weights.shape, f32),
            vm((3, rows, cols), f32),
            vm((rows, cols), f32),
            vm((rows, cols), f32),
            vm((rows, cols), i32),
            vm((lines, 128), i32),
            vm((lines, 128), i32),
            vm((5, tall, cols), f32),
            vm((tall, cols), f32),
            vm((SLABS, 5, 16, 128), f32),
            vm((SLABS, 5, 8, 128), f32),
            vm((SLABS, 5, 8, 128), f32),
            vm((5, PAD, cols), f32),
            vm((6, 5, PAD, cols), f32),
            vm((3, 128, cols), f32),
            vm((cols, 128), f32),
            vm((2, 8, 128), f32),
            vm((4, lines, 128), i32),
            vm((2 * ext, LOW * 128), f32),
            vm((ext, 128), f32),
            dma((6,)),
            dma((8,)),
            dma((8,)),
            dma((5,)),
        ],
        compiler_params=pltpu.CompilerParams(
            collective_id=0, has_side_effects=True, vmem_limit_bytes=56 * 1024 * 1024
        ),
        name="exchange",
    )(
        initial_state, bottom_drag, drag_direction, land_mask,
        section_cells.reshape(lines, 128), section_sign.reshape(lines, 128),
    )
    return pl.pallas_call(
        chain_kernel,
        out_shape=(
            jax.ShapeDtypeStruct((rows, cols), f32),
            jax.ShapeDtypeStruct((3, rows, cols), f32),
            jax.ShapeDtypeStruct((3, rows, cols), f32),
        ),
        in_specs=[hbm] * 3,
        out_specs=(hbm, hbm, hbm),
        scratch_shapes=[
            vm(fields.shape, f32),
            vm(patches.shape, f32),
            vm(weights.shape, f32),
            vm((ITERS, 6, SLABS, ext, 128), f32),
            vm((6, SLABS, ext, 128), f32),
            vm((6, SLABS, ext, 128), f32),
            vm((SLABS, ext, 128), f32),
            vm((SLABS, cols, 128), f32),
            vm((7, tall, cols), f32),
            dma((5,)),
            dma((7,)),
        ],
        compiler_params=pltpu.CompilerParams(vmem_limit_bytes=56 * 1024 * 1024),
        name="chain",
    )(fields, patches, weights)


def solution(mesh):
    return jax.shard_map(
        on_device,
        mesh=mesh,
        in_specs=(
            P(None, "lat", "lon"),
            P("lat", "lon"),
            P("lat", "lon"),
            P("lat", "lon"),
            P(),
            P(),
        ),
        out_specs=(P("lat", "lon"), P(None, "lat", "lon"), P(None, "lat", "lon")),
        check_vma=False,
    )
```

```python
import functools

import jax
import jax.numpy as jnp
from jax import lax
from jax.experimental import pallas as pl
from jax.experimental.pallas import tpu as pltpu
from jax.sharding import PartitionSpec as P

ITERS = 6
SLABS = 7
LOW = (SLABS + 1) // 2
PAD = 8
HALO_LANES = (17, 24, 49, 56, 81)
CHUNK = 8
MESH = pl.DeviceIdType.MESH


def patched(tile, halo_rows, f, j):
    lane = lax.broadcasted_iota(jnp.int32, tile.shape, 1)
    rolled = pltpu.roll(halo_rows, (128 - HALO_LANES[f] - j) % 128, 1)
    north = 111 if j < 4 else 110
    here = lane == 0 if j == 4 else (lane == 0) | (lane == north)
    return jnp.where(here, rolled, tile)


def exchange_kernel(
    init_hbm, drag_hbm, dir_hbm, mask_hbm, cells_hbm, sign_hbm,
    t_hbm, halo, from_west, from_east, w_hbm,
    t_ref, w_ref, init_ref, drag_ref, dir_ref, mask_ref, cells_ref, sign_ref,
    nat, edge, strip, north_tile, at_ref, acc, fold_acc, load_sem, send_sem, recv_sem, out_sem,
):
    rows, cols = drag_ref.shape
    ext = cols + 2 * PAD
    n_lon, n_lat = lax.axis_size("lon"), lax.axis_size("lat")
    lon, lat = lax.axis_index("lon"), lax.axis_index("lat")
    top = lat == n_lat - 1
    inner = lat > 0

    loads = [
        pltpu.make_async_copy(src, dst, load_sem.at[k])
        for k, (src, dst) in enumerate((
            (mask_hbm, mask_ref), (drag_hbm, drag_ref), (init_hbm, init_ref),
            (dir_hbm, dir_ref), (cells_hbm, cells_ref), (sign_hbm, sign_ref),
        ))
    ]
    def around(at, by):
        return lax.rem(at + by + n_lon, n_lon)

    up_lat = jnp.where(top, lat, lat + 1)
    up_lon = jnp.where(top, n_lon - 1 - lon, lon)
    up_slot = jnp.where(top, 3, 0)
    turns = (0, 1, -1)
    ups = [around(up_lon, by) for by in turns]
    downs = [around(lon, by) for by in turns]
    own_fold = [top & (at == lon) for at in ups]

    def device(lon_at, lat_at):
        return {"lon": lon_at, "lat": lat_at}

    barrier = pltpu.get_barrier_semaphore()

    def greet(lon_at, lat_at):
        pl.semaphore_signal(
            barrier, inc=1, device_id=device(lon_at, lat_at), device_id_type=MESH
        )

    greet(around(lon, 1), lat)
    greet(around(lon, -1), lat)
    peers = 2
    for k in range(3):
        pl.when(jnp.logical_not(own_fold[k]))(functools.partial(greet, ups[k], up_lat))
        pl.when(inner)(functools.partial(greet, downs[k], lat - 1))
        peers += jnp.where(own_fold[k], 0, 1) + jnp.where(inner, 1, 0)
    for load in loads:
        load.start()

    lane_of = lax.broadcasted_iota(jnp.int32, (64, cols), 1)

    def prepare(part, carry):
        here = pl.ds(pl.multiple_of(part * 64, 64), 64)
        there = pl.ds(pl.multiple_of(part * 64 + PAD, 8), 64)
        ocean = mask_ref[here, :].astype(jnp.float32)
        inverse = 1.0 / (1.0 + drag_ref[here, :])
        fields = [
            init_ref[0, here, :] * (0.2 * ocean),
            init_ref[1, here, :] * ocean,
            init_ref[2, here, :] * ocean,
            ocean * inverse,
            -(dir_ref[here, :] * inverse),
        ]
        sides = pltpu.roll(fields[0], 8, 1)
        for f in range(5):
            nat[f, there, :] = fields[f]
            if f:
                sides = jnp.where(
                    lane_of < 16 * f, sides, pltpu.roll(fields[f], 16 * f + 8, 1)
                )
        edge[there, :] = sides
        return carry

    height = nat.shape[1]
    tail = rows + PAD
    for f in range(5):
        nat[f, 0:PAD, :] = jnp.zeros((PAD, cols), jnp.float32)
        nat[f, tail:, :] = jnp.zeros((height - tail, cols), jnp.float32)
    edge[0:PAD, :] = jnp.zeros((PAD, cols), jnp.float32)
    edge[tail:, :] = jnp.zeros((height - tail, cols), jnp.float32)
    for load in loads[:4]:
        load.wait()
    lax.fori_loop(0, rows // 64, prepare, 0)

    @pl.when(jnp.logical_not(top))
    def _():
        north_tile[...] = nat[:, rows : rows + PAD, :]

    @pl.when(top)
    def _():
        lanes = lax.broadcasted_iota(jnp.int32, (PAD, cols), 1)
        for f in range(5):
            tile = nat[f, rows : rows + PAD, :]
            turned = jnp.take_along_axis(tile, cols - 1 - lanes, axis=1)
            if f in (1, 2):
                turned = -turned
            for k in range(PAD):
                north_tile[f, k : k + 1, :] = turned[PAD - 1 - k : PAD - k, :]

    def fill(src, slot):
        return pltpu.make_async_copy(src, halo.at[slot], out_sem.at[2 + slot])

    zeros = nat.at[:, pl.ds(tail, PAD), :]
    lowest = jnp.logical_not(inner)
    for k in range(3):
        pl.when(lowest)(fill(zeros, k).start)
        pl.when(own_fold[k])(fill(north_tile, 3 + k).start)

    for j in range(SLABS):
        turned = edge[pl.ds(j + 1, 128, stride=SLABS), :].T
        for f in range(5):
            strip[j, f] = turned[16 * f : 16 * f + 16]

    def copy(src, dst, which, slot, lon_at, lat_at):
        return pltpu.make_async_remote_copy(
            src_ref=src, dst_ref=dst, send_sem=send_sem.at[which],
            recv_sem=recv_sem.at[slot], device_id=device(lon_at, lat_at),
            device_id_type=MESH,
        )

    up_copies = [
        copy(north_tile, halo.at[up_slot + k], k, up_slot + k, ups[k], up_lat)
        for k in range(3)
    ]
    down_copies = [
        copy(nat.at[:, pl.ds(PAD, PAD), :], halo.at[3 + k], 3 + k, 3 + k, downs[k], lat - 1)
        for k in range(3)
    ]
    east_copy = copy(
        strip.at[:, pl.ds(0, 5), pl.ds(0, 8), :], from_west, 6, 6, around(lon, 1), lat
    )
    west_copy = copy(
        strip.at[:, pl.ds(0, 5), pl.ds(8, 8), :], from_east, 7, 7, around(lon, -1), lat
    )

    pl.semaphore_wait(barrier, peers)
    east_copy.start()
    west_copy.start()
    for k in (1, 2, 0):
        pl.when(jnp.logical_not(own_fold[k]))(up_copies[k].start)
        pl.when(inner)(down_copies[k].start)

    for f in range(5):
        for j in range(SLABS):
            t_ref[f, j] = nat[f, pl.ds(j + 1, 128, stride=SLABS), :].T
    own_out = pltpu.make_async_copy(t_ref, t_hbm, out_sem.at[0])
    own_out.start()
    for load in loads[4:]:
        load.wait()

    total = cols * n_lon
    cell = cells_ref[...]
    row, col = lax.div(cell, total), lax.rem(cell, total)
    r = row - lat * rows + SLABS
    lane = lax.shift_right_arithmetic(r * 9363, 16)
    slab = r - lane * SLABS
    c = col - lon * cols + PAD
    c = jnp.where(c < 0, c + total, c)
    c = jnp.where(c >= total, c - total, c)
    in_rows = (r >= 0) & (r < rows + 2 * SLABS)
    at_ref[0] = jnp.where(c < ext, lax.div(slab, LOW) * ext + c, -1)
    at_ref[1] = jnp.where(in_rows, lax.rem(slab, LOW) * 128 + lane, -1)
    fr = rows - 1 - (row - lat * rows)
    at_ref[2] = jnp.where(top & (fr < SLABS), fr, -1)
    fc = total - 1 - col - lon * cols + PAD
    fc = jnp.where(fc < 0, fc + total, fc)
    at_ref[3] = jnp.where(fc >= total, fc - total, fc)

    contract = (((1,), (1,)), ((), ()))
    acc[...] = jnp.zeros_like(acc)
    fold_acc[...] = jnp.zeros_like(fold_acc)

    def spread(which, at):
        line = at_ref[which, pl.ds(at, 1), :]
        return jnp.broadcast_to(line, (16, 128)).astype(jnp.int16)

    def one_hot(which, first, size, value=None):
        steps = lax.broadcasted_iota(jnp.int16, (size, 128), 0)
        found = []
        for k in range(CHUNK):
            at = jnp.concatenate([spread(which, first + k)] * (size // 16), axis=0)
            if value is None:
                hit = jnp.ones((size, 128), jnp.bfloat16)
            else:
                hit = jnp.concatenate([value[k]] * (size // 16), axis=0)
            found.append(jnp.where(steps == at, hit, jnp.zeros((size, 128), jnp.bfloat16)))
        return jnp.concatenate(found, axis=1)

    def gather_weights(part, carry):
        first = part * CHUNK
        signs = [
            jnp.broadcast_to(sign_ref[pl.ds(first + k, 1), :], (16, 128))
            .astype(jnp.float32).astype(jnp.bfloat16)
            for k in range(CHUNK)
        ]
        a = one_hot(0, first, 2 * ext)
        b = one_hot(1, first, LOW * 128, signs)
        acc[...] += lax.dot_general(a, b, contract, preferred_element_type=jnp.float32)
        fa = one_hot(3, first, ext)
        fb = one_hot(2, first, 16, signs)
        fold_acc[:, 0:16] += lax.dot_general(
            fa, fb, contract, preferred_element_type=jnp.float32
        )
        return carry

    lax.fori_loop(0, cells_ref.shape[0] // CHUNK, gather_weights, 0)
    column = lax.broadcasted_iota(jnp.int32, (ext, 128), 1)
    ghosts = fold_acc[...]
    for j in range(SLABS):
        hi, lo = divmod(j, LOW)
        found = acc[hi * ext : (hi + 1) * ext, lo * 128 : (lo + 1) * 128]
        for k in range(SLABS):
            lane_at, slab_at = divmod(rows + SLABS + k, SLABS)
            if slab_at == j:
                turned = pltpu.roll(ghosts, lane_at - k, 1)
                found -= jnp.where(column == lane_at, turned, 0.0)
        w_ref[j] = found
    w_out = pltpu.make_async_copy(w_ref, w_hbm, out_sem.at[1])
    w_out.start()

    for k in range(3):
        pl.when(inner)(
            copy(north_tile, halo.at[k], k, k, ups[k], up_lat).wait_recv
        )
        pl.when(jnp.logical_not(own_fold[k]))(
            copy(north_tile, halo.at[3 + k], k, 3 + k, ups[k], up_lat).wait_recv
        )
        pl.when(lowest)(fill(zeros, k).wait)
        pl.when(own_fold[k])(fill(north_tile, 3 + k).wait)
        pl.when(jnp.logical_not(own_fold[k]))(up_copies[k].wait_send)
        pl.when(inner)(down_copies[k].wait_send)
    east_copy.wait_send()
    west_copy.wait_send()
    own_out.wait()
    w_out.wait()
    east_copy.wait_recv()
    west_copy.wait_recv()


def chain_kernel(
    t_hbm, halo_hbm, west_hbm, east_hbm, w_hbm, curv_hbm, state_hbm, tangent_hbm,
    t_ref, halo, from_west, from_east, pack, patch, w_ref, levels, back_a, back_b, scale_ref, curv, nat, load_sem, out_sem,
):
    ext = t_ref.shape[2]
    cols = ext - 2 * PAD
    rows = curv_hbm.shape[0]
    tiles = ext // 8
    bounds = (0, 16, 64, cols)
    sides = [
        pltpu.make_async_copy(src, dst, load_sem.at[k])
        for k, (src, dst) in enumerate((
            (halo_hbm, halo), (west_hbm, from_west), (east_hbm, from_east)
        ))
    ]
    loads = [
        pltpu.make_async_copy(
            t_hbm.at[:, :, pl.ds(low, high - low), :],
            t_ref.at[:, :, pl.ds(PAD + low, high - low), :], load_sem.at[3 + k],
        )
        for k, (low, high) in enumerate(zip(bounds, bounds[1:]))
    ]
    w_load = pltpu.make_async_copy(w_hbm, w_ref, load_sem.at[6])
    for load in sides + loads + [w_load]:
        load.start()

    def around(src, field, j, i):
        if i == 0:
            low = pltpu.roll(src[field, j, 0:8, :], 1, 0)
        else:
            low = src[field, j, 8 * i - 1 : 8 * i + 7, :]
        if i == tiles - 1:
            high = pltpu.roll(src[field, j, 8 * i : 8 * i + 8, :], 7, 0)
        else:
            high = src[field, j, 8 * i + 1 : 8 * i + 9, :]
        return high - low

    def step(src, dst, i, spin, use=None, first=False):
        here = slice(8 * i, 8 * i + 8)
        parts = (0,) if first else (0, 3)

        def get(field, j):
            return src[field, j, here, :]

        up = {f: pltpu.roll(get(f, 0), 127, 1) for p in parts for f in (p, p + 2)}
        before = {f: pltpu.roll(get(f, SLABS - 1), 1, 1) for p in parts for f in (p, p + 2)}
        now = {f: get(f, 0) for p in parts for f in (p, p + 2)}
        for j in range(SLABS):
            damp, factor = t_ref[3, j, here, :], t_ref[4, j, here, :]
            if first:
                scale = jnp.where(damp > 0.0, 0.04, 0.0)
                scale_ref[j, here, :] = scale
            else:
                scale = scale_ref[j, here, :]
            after = {
                f: get(f, j + 1) if j < SLABS - 1 else up[f] for p in parts for f in (p, p + 2)
            }
            new = []
            for p in parts:
                h, u, v = p, p + 1, p + 2
                um, vm = get(u, j), now[v]
                new_h = now[h] - scale * (around(src, u, j, i) + (after[v] - before[v]))
                new_u = (um - around(src, h, j, i) + spin * vm) * damp
                new_v = (vm - (after[h] - before[h]) - spin * um) * damp
                if p:
                    new_u += factor * new[0]
                    new_v += factor * new[1]
                new += [new_u, new_v]
                dst[h, j, here, :] = new_h
                dst[u, j, here, :] = new_u
                dst[v, j, here, :] = new_v
            if first:
                new += [factor * new[0], factor * new[1]]
                dst[3, j, here, :] = jnp.zeros((8, 128), jnp.float32)
                dst[4, j, here, :] = new[2]
                dst[5, j, here, :] = new[3]
            if use is not None:
                use(j, i, here, new)
            before, now = now, after

    def weigh(level):
        def use(j, i, here, new):
            if 0 < i < tiles - 1:
                qu, qv, ru, rv = new
                own = slice(8 * i - 8, 8 * i)
                curv[j, own, :] -= (
                    level[4, j, here, :] * qu + level[5, j, here, :] * qv
                ) + (level[1, j, here, :] * ru + level[2, j, here, :] * rv)
        return use

    def turn(field, times=None):
        for j in range(SLABS):
            block = levels[ITERS - 1, field, j, PAD : PAD + cols, :]
            if times is not None:
                block = block * times
            nat[field, pl.ds(j + 1, 128, stride=SLABS), :] = block.T

    def send(field, out, at):
        return pltpu.make_async_copy(
            nat.at[field, pl.ds(PAD, rows), :], out.at[at], out_sem.at[field]
        )

    pack[...] = jnp.zeros_like(pack)
    sides[0].wait()
    for k in range(3):
        for f in range(5):
            at = HALO_LANES[f]
            pack[k, at : at + 7, :] = halo[k, f, 1:8, :]
            pack[k, at - 17 : at - 13, :] = halo[3 + k, f, 2:6, :]
            pack[k, at - 13 : at - 11, :] = halo[3 + k, f, 0:2, :]
    patch[...] = pack[0].T
    corners = pack[1].T[cols - PAD : cols], pack[2].T[0:PAD]
    sides[1].wait()
    sides[2].wait()
    for got, corner, place in zip((from_west, from_east), corners, (0, cols + PAD)):
        for f in range(5):
            for j in range(SLABS):
                t_ref[f, j, place : place + PAD, :] = patched(got[j, f], corner, f, j)

    for i in range(tiles):
        for load, low in zip(loads, bounds):
            if 8 * i == low:
                load.wait()
        if i < tiles - 2:
            here = slice(8 * i + PAD, 8 * i + PAD + 8)
            halo_rows = patch[8 * i : 8 * i + 8, :]
            for f in range(5):
                for j in range(SLABS):
                    t_ref[f, j, here, :] = patched(t_ref[f, j, here, :], halo_rows, f, j)
        step(t_ref, levels.at[0], i, 0.25, first=True)

    def forward(n, carry):
        for i in range(tiles):
            step(levels.at[n], levels.at[n + 1], i, 0.25)
        return carry

    lax.fori_loop(0, ITERS - 1, forward, 0)

    w_load.wait()
    last, prior = levels.at[ITERS - 1], levels.at[ITERS - 2]
    for i in range(tiles):
        here = slice(8 * i, 8 * i + 8)
        q = [t_ref[3, j, here, :] * w_ref[j, here, :] for j in range(SLABS)]
        r = [t_ref[4, j, here, :] * q[j] for j in range(SLABS)]
        q = [pltpu.roll(q[-1], 1, 1)] + q + [pltpu.roll(q[0], 127, 1)]
        r = [pltpu.roll(r[-1], 1, 1)] + r + [pltpu.roll(r[0], 127, 1)]
        for j in range(SLABS):
            damp, factor = t_ref[3, j, here, :], t_ref[4, j, here, :]
            scale = scale_ref[j, here, :]
            qv, rv = q[j + 1] * damp, r[j + 1] * damp
            qu, ru = -0.25 * qv, -0.25 * rv
            rv, ru = rv + factor * qv, ru + factor * qu
            back_a[0, j, here, :] = scale * (q[j] - q[j + 2])
            back_a[1, j, here, :] = qu
            back_a[2, j, here, :] = qv
            back_a[3, j, here, :] = scale * (r[j] - r[j + 2])
            back_a[4, j, here, :] = ru
            back_a[5, j, here, :] = rv
            if 0 < i < tiles - 1:
                done = last[5, j, here, :] * q[j + 1] + last[2, j, here, :] * r[j + 1]
                done += prior[4, j, here, :] * qu + prior[5, j, here, :] * qv
                done += prior[1, j, here, :] * ru + prior[2, j, here, :] * rv
                curv[j, 8 * i - 8 : 8 * i, :] = -done
    turn(0, 5.0)
    turn(3, 5.0)
    send(0, state_hbm, 0).start()
    send(3, tangent_hbm, 0).start()

    def backward(k, carry):
        turn(1 + k)
        for i in range(tiles):
            step(back_a, back_b, i, -0.25, weigh(levels.at[ITERS - 3 - 2 * k]))
        send(1 + k, state_hbm, 1 + k).start()
        turn(4 + k)
        for i in range(tiles):
            step(back_b, back_a, i, -0.25, weigh(levels.at[ITERS - 4 - 2 * k]))
        send(4 + k, tangent_hbm, 1 + k).start()
        return carry

    lax.fori_loop(0, (ITERS - 2) // 2, backward, 0)
    for j in range(SLABS):
        nat[6, pl.ds(j + 1, 128, stride=SLABS), :] = curv[j].T
    curv_copy = pltpu.make_async_copy(nat.at[6, pl.ds(PAD, rows), :], curv_hbm, out_sem.at[6])
    curv_copy.start()
    for f in range(3):
        send(f, state_hbm, f).wait()
        send(3 + f, tangent_hbm, f).wait()
    curv_copy.wait()


def on_device(initial_state, bottom_drag, drag_direction, land_mask, section_cells, section_sign):
    rows, cols = bottom_drag.shape
    ext = cols + 2 * PAD
    f32, i32 = jnp.float32, jnp.int32
    hbm = pl.BlockSpec(memory_space=pl.ANY)
    lines = section_cells.shape[0] // 128
    tall = SLABS * 128 + 8
    vm, dma = pltpu.VMEM, pltpu.SemaphoreType.DMA
    fields = jax.ShapeDtypeStruct((5, SLABS, cols, 128), f32)
    halos = jax.ShapeDtypeStruct((6, 5, PAD, cols), f32)
    beside = jax.ShapeDtypeStruct((SLABS, 5, PAD, 128), f32)
    weights = jax.ShapeDtypeStruct((SLABS, ext, 128), f32)
    given = pl.pallas_call(
        exchange_kernel,
        out_shape=(fields, halos, beside, beside, weights),
        in_specs=[hbm] * 6,
        out_specs=(hbm,) * 5,
        scratch_shapes=[
            vm(fields.shape, f32),
            vm(weights.shape, f32),
            vm((3, rows, cols), f32),
            vm((rows, cols), f32),
            vm((rows, cols), f32),
            vm((rows, cols), i32),
            vm((lines, 128), i32),
            vm((lines, 128), i32),
            vm((5, tall, cols), f32),
            vm((tall, cols), f32),
            vm((SLABS, 5, 16, 128), f32),
            vm((5, PAD, cols), f32),
            vm((4, lines, 128), i32),
            vm((2 * ext, LOW * 128), f32),
            vm((ext, 128), f32),
            dma((6,)),
            dma((8,)),
            dma((8,)),
            dma((8,)),
        ],
        compiler_params=pltpu.CompilerParams(
            collective_id=0, has_side_effects=True, vmem_limit_bytes=56 * 1024 * 1024
        ),
        name="exchange",
    )(
        initial_state, bottom_drag, drag_direction, land_mask,
        section_cells.reshape(lines, 128), section_sign.reshape(lines, 128),
    )
    return pl.pallas_call(
        chain_kernel,
        out_shape=(
            jax.ShapeDtypeStruct((rows, cols), f32),
            jax.ShapeDtypeStruct((3, rows, cols), f32),
            jax.ShapeDtypeStruct((3, rows, cols), f32),
        ),
        in_specs=[hbm] * 5,
        out_specs=(hbm, hbm, hbm),
        scratch_shapes=[
            vm((5, SLABS, ext, 128), f32),
            vm(halos.shape, f32),
            vm(beside.shape, f32),
            vm(beside.shape, f32),
            vm((3, 128, cols), f32),
            vm((cols, 128), f32),
            vm(weights.shape, f32),
            vm((ITERS, 6, SLABS, ext, 128), f32),
            vm((6, SLABS, ext, 128), f32),
            vm((6, SLABS, ext, 128), f32),
            vm((SLABS, ext, 128), f32),
            vm((SLABS, cols, 128), f32),
            vm((7, tall, cols), f32),
            dma((7,)),
            dma((7,)),
        ],
        compiler_params=pltpu.CompilerParams(vmem_limit_bytes=56 * 1024 * 1024),
        name="chain",
    )(*given)


def solution(mesh):
    return jax.shard_map(
        on_device,
        mesh=mesh,
        in_specs=(
            P(None, "lat", "lon"),
            P("lat", "lon"),
            P("lat", "lon"),
            P("lat", "lon"),
            P(),
            P(),
        ),
        out_specs=(P("lat", "lon"), P(None, "lat", "lon"), P(None, "lat", "lon")),
        check_vma=False,
    )
```

```python
import functools

import jax
import jax.numpy as jnp
from jax import lax
from jax.experimental import pallas as pl
from jax.experimental.pallas import tpu as pltpu
from jax.sharding import PartitionSpec as P

ITERS = 6
SLABS = 7
LOW = (SLABS + 1) // 2
PAD = 8
HALO_LANES = (17, 24, 49, 56, 81)
CHUNK = 8
MESH = pl.DeviceIdType.MESH


def patched(tile, halo_rows, at, j):
    lane = lax.broadcasted_iota(jnp.int32, tile.shape, 1)
    rolled = pltpu.roll(halo_rows, (128 - at - j) % 128, 1)
    north = 111 if j < 4 else 110
    here = lane == 0 if j == 4 else (lane == 0) | (lane == north)
    return jnp.where(here, rolled, tile)


def exchange_kernel(
    init_hbm, drag_hbm, dir_hbm, mask_hbm, cells_hbm, sign_hbm,
    t_hbm, halo, corner, from_west, from_east, w_hbm,
    t_ref, w_ref, init_ref, drag_ref, dir_ref, mask_ref, cells_ref, sign_ref,
    nat, north_tile, edge_tile, at_ref, acc, fold_acc, load_sem, send_sem, recv_sem, out_sem,
):
    rows, cols = drag_ref.shape
    ext = cols + 2 * PAD
    n_lon, n_lat = lax.axis_size("lon"), lax.axis_size("lat")
    lon, lat = lax.axis_index("lon"), lax.axis_index("lat")
    top = lat == n_lat - 1
    inner = lat > 0

    loads = [
        pltpu.make_async_copy(src, dst, load_sem.at[k])
        for k, (src, dst) in enumerate((
            (mask_hbm, mask_ref), (drag_hbm, drag_ref), (init_hbm, init_ref),
            (dir_hbm, dir_ref), (cells_hbm, cells_ref), (sign_hbm, sign_ref),
        ))
    ]
    def around(at, by):
        return lax.rem(at + by + n_lon, n_lon)

    up_lat = jnp.where(top, lat, lat + 1)
    up_lon = jnp.where(top, n_lon - 1 - lon, lon)
    up_half = jnp.where(top, 1, 0)
    turns = (0, 1, -1)
    ups = [around(up_lon, by) for by in turns]
    downs = [around(lon, by) for by in turns]
    own_fold = [top & (at == lon) for at in ups]

    def device(lon_at, lat_at):
        return {"lon": lon_at, "lat": lat_at}

    barrier = pltpu.get_barrier_semaphore()

    def greet(lon_at, lat_at):
        pl.semaphore_signal(
            barrier, inc=1, device_id=device(lon_at, lat_at), device_id_type=MESH
        )

    greet(around(lon, 1), lat)
    greet(around(lon, -1), lat)
    peers = 2
    for k in range(3):
        pl.when(jnp.logical_not(own_fold[k]))(functools.partial(greet, ups[k], up_lat))
        pl.when(inner)(functools.partial(greet, downs[k], lat - 1))
        peers += jnp.where(own_fold[k], 0, 1) + jnp.where(inner, 1, 0)
    for load in loads:
        load.start()

    def beside(fields):
        lane_of = lax.broadcasted_iota(jnp.int32, fields[0].shape, 1)
        sides = pltpu.roll(fields[0], 8, 1)
        for f in range(1, 5):
            sides = jnp.where(lane_of < 16 * f, sides, pltpu.roll(fields[f], 16 * f + 8, 1))
        return sides

    def prepare(part, carry):
        here = pl.ds(pl.multiple_of(part * 64, 64), 64)
        there = pl.ds(pl.multiple_of(part * 64 + PAD, 8), 64)
        ocean = mask_ref[here, :].astype(jnp.float32)
        inverse = 1.0 / (1.0 + drag_ref[here, :])
        fields = [
            init_ref[0, here, :] * (0.2 * ocean),
            init_ref[1, here, :] * ocean,
            init_ref[2, here, :] * ocean,
            ocean * inverse,
            -(dir_ref[here, :] * inverse),
        ]
        for f in range(5):
            nat[f, there, :] = fields[f]
        return carry

    height = nat.shape[1]
    tail = rows + PAD
    for f in range(5):
        nat[f, 0:PAD, :] = jnp.zeros((PAD, cols), jnp.float32)
        nat[f, tail:, :] = jnp.zeros((height - tail, cols), jnp.float32)
    for load in loads[:4]:
        load.wait()
    lax.fori_loop(0, rows // 64, prepare, 0)

    @pl.when(jnp.logical_not(top))
    def _():
        north_tile[...] = nat[:, rows : rows + PAD, :]

    @pl.when(top)
    def _():
        lanes = lax.broadcasted_iota(jnp.int32, (PAD, cols), 1)
        for f in range(5):
            tile = nat[f, rows : rows + PAD, :]
            turned = jnp.take_along_axis(tile, cols - 1 - lanes, axis=1)
            if f in (1, 2):
                turned = -turned
            for k in range(PAD):
                north_tile[f, k : k + 1, :] = turned[PAD - 1 - k : PAD - k, :]

    edge_tile[0] = beside([north_tile[f] for f in range(5)])
    edge_tile[1] = beside([nat[f, PAD : 2 * PAD, :] for f in range(5)])

    def fill(src, dst, which):
        return pltpu.make_async_copy(src, dst, out_sem.at[which])

    lowest = jnp.logical_not(inner)
    fills = [(lowest, fill(nat.at[:, pl.ds(tail, PAD), :], halo.at[0], 2))]
    for k in range(2):
        fills.append((lowest, fill(nat.at[0, pl.ds(tail, PAD), :], corner.at[k], 3 + k)))
        fills.append((own_fold[1 + k], fill(edge_tile.at[0], corner.at[2 + k], 5 + k)))
    for case, part in fills:
        pl.when(case)(part.start)

    def copy(src, dst, which, slot, lon_at, lat_at):
        return pltpu.make_async_remote_copy(
            src_ref=src, dst_ref=dst, send_sem=send_sem.at[which],
            recv_sem=recv_sem.at[slot], device_id=device(lon_at, lat_at),
            device_id_type=MESH,
        )

    up_copies = [copy(north_tile, halo.at[up_half], 0, up_half, ups[0], up_lat)]
    down_copies = [
        copy(nat.at[:, pl.ds(PAD, PAD), :], halo.at[1], 3, 1, downs[0], lat - 1)
    ]
    for k in range(2):
        slot = 2 * up_half + k
        up_copies.append(
            copy(edge_tile.at[0], corner.at[slot], 1 + k, 2 + slot, ups[1 + k], up_lat)
        )
        down_copies.append(
            copy(
                edge_tile.at[1], corner.at[2 + k], 4 + k, 4 + k,
                downs[1 + k], lat - 1,
            )
        )
    east_copy = copy(
        t_ref.at[:, :, pl.ds(cols - PAD, PAD), :], from_west, 6, 6, around(lon, 1), lat
    )
    west_copy = copy(
        t_ref.at[:, :, pl.ds(0, PAD), :], from_east, 7, 7, around(lon, -1), lat
    )

    for f in range(5):
        for j in range(SLABS):
            t_ref[f, j] = nat[f, pl.ds(j + 1, 128, stride=SLABS), :].T
    own_out = pltpu.make_async_copy(t_ref, t_hbm, out_sem.at[0])
    own_out.start()

    pl.semaphore_wait(barrier, peers)
    for k in (1, 2, 0):
        pl.when(jnp.logical_not(own_fold[k]))(up_copies[k].start)
        pl.when(inner)(down_copies[k].start)
    east_copy.start()
    west_copy.start()
    for load in loads[4:]:
        load.wait()

    total = cols * n_lon
    cell = cells_ref[...]
    row, col = lax.div(cell, total), lax.rem(cell, total)
    r = row - lat * rows + SLABS
    lane = lax.shift_right_arithmetic(r * 9363, 16)
    slab = r - lane * SLABS
    c = col - lon * cols + PAD
    c = jnp.where(c < 0, c + total, c)
    c = jnp.where(c >= total, c - total, c)
    in_rows = (r >= 0) & (r < rows + 2 * SLABS)
    at_ref[0] = jnp.where(c < ext, lax.div(slab, LOW) * ext + c, -1)
    at_ref[1] = jnp.where(in_rows, lax.rem(slab, LOW) * 128 + lane, -1)
    fr = rows - 1 - (row - lat * rows)
    at_ref[2] = jnp.where(top & (fr < SLABS), fr, -1)
    fc = total - 1 - col - lon * cols + PAD
    fc = jnp.where(fc < 0, fc + total, fc)
    at_ref[3] = jnp.where(fc >= total, fc - total, fc)

    contract = (((1,), (1,)), ((), ()))
    acc[...] = jnp.zeros_like(acc)
    fold_acc[...] = jnp.zeros_like(fold_acc)

    def spread(which, at):
        line = at_ref[which, pl.ds(at, 1), :]
        return jnp.broadcast_to(line, (16, 128)).astype(jnp.int16)

    def one_hot(which, first, size, value=None):
        steps = lax.broadcasted_iota(jnp.int16, (size, 128), 0)
        found = []
        for k in range(CHUNK):
            at = jnp.concatenate([spread(which, first + k)] * (size // 16), axis=0)
            if value is None:
                hit = jnp.ones((size, 128), jnp.bfloat16)
            else:
                hit = jnp.concatenate([value[k]] * (size // 16), axis=0)
            found.append(jnp.where(steps == at, hit, jnp.zeros((size, 128), jnp.bfloat16)))
        return jnp.concatenate(found, axis=1)

    def signs_of(first):
        return [
            jnp.broadcast_to(sign_ref[pl.ds(first + k, 1), :], (16, 128))
            .astype(jnp.float32).astype(jnp.bfloat16)
            for k in range(CHUNK)
        ]

    def gather_weights(part, carry):
        first = part * CHUNK
        signs = signs_of(first)
        a = one_hot(0, first, 2 * ext)
        b = one_hot(1, first, LOW * 128, signs)
        acc[...] += lax.dot_general(a, b, contract, preferred_element_type=jnp.float32)
        return carry

    lax.fori_loop(0, cells_ref.shape[0] // CHUNK, gather_weights, 0)

    @pl.when(top)
    def _():
        def gather_ghosts(part, carry):
            first = part * CHUNK
            signs = signs_of(first)
            fa = one_hot(3, first, ext)
            fb = one_hot(2, first, 16, signs)
            fold_acc[:, 0:16] += lax.dot_general(
                fa, fb, contract, preferred_element_type=jnp.float32
            )
            return carry

        lax.fori_loop(0, cells_ref.shape[0] // CHUNK, gather_ghosts, 0)

    column = lax.broadcasted_iota(jnp.int32, (ext, 128), 1)
    ghosts = fold_acc[...]
    for j in range(SLABS):
        hi, lo = divmod(j, LOW)
        found = acc[hi * ext : (hi + 1) * ext, lo * 128 : (lo + 1) * 128]
        for k in range(SLABS):
            lane_at, slab_at = divmod(rows + SLABS + k, SLABS)
            if slab_at == j:
                turned = pltpu.roll(ghosts, lane_at - k, 1)
                found -= jnp.where(column == lane_at, turned, 0.0)
        w_ref[j] = found
    w_out = pltpu.make_async_copy(w_ref, w_hbm, out_sem.at[1])
    w_out.start()

    pl.when(inner)(copy(north_tile, halo.at[0], 0, 0, ups[0], up_lat).wait_recv)
    copy(north_tile, halo.at[1], 0, 1, ups[0], up_lat).wait_recv()
    for k in range(2):
        pl.when(inner)(
            copy(edge_tile.at[0], corner.at[k], 1 + k, 2 + k, ups[1 + k], up_lat).wait_recv
        )
        pl.when(jnp.logical_not(own_fold[1 + k]))(
            copy(edge_tile.at[0], corner.at[2 + k], 1 + k, 4 + k, ups[1 + k], up_lat).wait_recv
        )
    for case, part in fills:
        pl.when(case)(part.wait)
    for k in range(3):
        pl.when(jnp.logical_not(own_fold[k]))(up_copies[k].wait_send)
        pl.when(inner)(down_copies[k].wait_send)
    east_copy.wait_send()
    west_copy.wait_send()
    own_out.wait()
    w_out.wait()
    east_copy.wait_recv()
    west_copy.wait_recv()


def chain_kernel(
    t_hbm, halo_hbm, corner_hbm, west_hbm, east_hbm, w_hbm, curv_hbm, state_hbm, tangent_hbm,
    t_ref, halo, corner, from_west, from_east, pack, patch, w_ref, levels, back_a, back_b, scale_ref, curv, nat, load_sem, out_sem,
):
    ext = t_ref.shape[2]
    cols = ext - 2 * PAD
    rows = curv_hbm.shape[0]
    tiles = ext // 8
    bounds = (0, 16, 64, cols)
    sides = [
        pltpu.make_async_copy(src, dst, load_sem.at[k])
        for k, (src, dst) in enumerate((
            (halo_hbm, halo), (corner_hbm, corner), (west_hbm, from_west), (east_hbm, from_east)
        ))
    ]
    loads = [
        pltpu.make_async_copy(
            t_hbm.at[:, :, pl.ds(low, high - low), :],
            t_ref.at[:, :, pl.ds(PAD + low, high - low), :], load_sem.at[4 + k],
        )
        for k, (low, high) in enumerate(zip(bounds, bounds[1:]))
    ]
    w_load = pltpu.make_async_copy(w_hbm, w_ref, load_sem.at[7])
    for load in sides + loads + [w_load]:
        load.start()

    def around(src, field, j, i):
        if i == 0:
            low = pltpu.roll(src[field, j, 0:8, :], 1, 0)
        else:
            low = src[field, j, 8 * i - 1 : 8 * i + 7, :]
        if i == tiles - 1:
            high = pltpu.roll(src[field, j, 8 * i : 8 * i + 8, :], 7, 0)
        else:
            high = src[field, j, 8 * i + 1 : 8 * i + 9, :]
        return high - low

    def step(src, dst, i, spin, use=None, first=False):
        here = slice(8 * i, 8 * i + 8)
        parts = (0,) if first else (0, 3)

        def get(field, j):
            return src[field, j, here, :]

        up = {f: pltpu.roll(get(f, 0), 127, 1) for p in parts for f in (p, p + 2)}
        before = {f: pltpu.roll(get(f, SLABS - 1), 1, 1) for p in parts for f in (p, p + 2)}
        now = {f: get(f, 0) for p in parts for f in (p, p + 2)}
        for j in range(SLABS):
            damp, factor = t_ref[3, j, here, :], t_ref[4, j, here, :]
            if first:
                scale = jnp.where(damp > 0.0, 0.04, 0.0)
                scale_ref[j, here, :] = scale
            else:
                scale = scale_ref[j, here, :]
            after = {
                f: get(f, j + 1) if j < SLABS - 1 else up[f] for p in parts for f in (p, p + 2)
            }
            new = []
            for p in parts:
                h, u, v = p, p + 1, p + 2
                um, vm = get(u, j), now[v]
                new_h = now[h] - scale * (around(src, u, j, i) + (after[v] - before[v]))
                new_u = (um - around(src, h, j, i) + spin * vm) * damp
                new_v = (vm - (after[h] - before[h]) - spin * um) * damp
                if p:
                    new_u += factor * new[0]
                    new_v += factor * new[1]
                new += [new_u, new_v]
                dst[h, j, here, :] = new_h
                dst[u, j, here, :] = new_u
                dst[v, j, here, :] = new_v
            if first:
                new += [factor * new[0], factor * new[1]]
                dst[3, j, here, :] = jnp.zeros((8, 128), jnp.float32)
                dst[4, j, here, :] = new[2]
                dst[5, j, here, :] = new[3]
            if use is not None:
                use(j, i, here, new)
            before, now = now, after

    def weigh(level):
        def use(j, i, here, new):
            if 0 < i < tiles - 1:
                qu, qv, ru, rv = new
                own = slice(8 * i - 8, 8 * i)
                curv[j, own, :] -= (
                    level[4, j, here, :] * qu + level[5, j, here, :] * qv
                ) + (level[1, j, here, :] * ru + level[2, j, here, :] * rv)
        return use

    def turn(field, times=None):
        for j in range(SLABS):
            block = levels[ITERS - 1, field, j, PAD : PAD + cols, :]
            if times is not None:
                block = block * times
            nat[field, pl.ds(j + 1, 128, stride=SLABS), :] = block.T

    def send(field, out, at):
        return pltpu.make_async_copy(
            nat.at[field, pl.ds(PAD, rows), :], out.at[at], out_sem.at[field]
        )

    pack[...] = jnp.zeros_like(pack)
    sides[0].wait()
    sides[1].wait()

    def place_rows(k, at, south, north):
        pack[k, at : at + 7, :] = south[1:8]
        pack[k, at - 17 : at - 13, :] = north[2:6]
        pack[k, at - 13 : at - 11, :] = north[0:2]

    for f in range(5):
        place_rows(0, HALO_LANES[f], halo[0, f], halo[1, f])
    for k in range(2):
        place_rows(1 + k, HALO_LANES[0], corner[k], corner[2 + k])
    patch[...] = pack[0].T
    corners = pack[1].T, pack[2].T
    sides[2].wait()
    sides[3].wait()
    for k, (got, place) in enumerate(((from_west, 0), (from_east, cols + PAD))):
        for f in range(5):
            rows_in = corners[k][16 * f + 8 * k : 16 * f + 8 * k + 8]
            for j in range(SLABS):
                t_ref[f, j, place : place + PAD, :] = patched(
                    got[f, j], rows_in, HALO_LANES[0], j
                )

    for i in range(tiles):
        for load, low in zip(loads, bounds):
            if 8 * i == low:
                load.wait()
        if i < tiles - 2:
            here = slice(8 * i + PAD, 8 * i + PAD + 8)
            halo_rows = patch[8 * i : 8 * i + 8, :]
            for f in range(5):
                for j in range(SLABS):
                    t_ref[f, j, here, :] = patched(
                        t_ref[f, j, here, :], halo_rows, HALO_LANES[f], j
                    )
        step(t_ref, levels.at[0], i, 0.25, first=True)

    def forward(n, carry):
        for i in range(tiles):
            step(levels.at[n], levels.at[n + 1], i, 0.25)
        return carry

    lax.fori_loop(0, ITERS - 1, forward, 0)

    w_load.wait()
    last, prior = levels.at[ITERS - 1], levels.at[ITERS - 2]
    for i in range(tiles):
        here = slice(8 * i, 8 * i + 8)
        q = [t_ref[3, j, here, :] * w_ref[j, here, :] for j in range(SLABS)]
        r = [t_ref[4, j, here, :] * q[j] for j in range(SLABS)]
        q = [pltpu.roll(q[-1], 1, 1)] + q + [pltpu.roll(q[0], 127, 1)]
        r = [pltpu.roll(r[-1], 1, 1)] + r + [pltpu.roll(r[0], 127, 1)]
        for j in range(SLABS):
            damp, factor = t_ref[3, j, here, :], t_ref[4, j, here, :]
            scale = scale_ref[j, here, :]
            qv, rv = q[j + 1] * damp, r[j + 1] * damp
            qu, ru = -0.25 * qv, -0.25 * rv
            rv, ru = rv + factor * qv, ru + factor * qu
            back_a[0, j, here, :] = scale * (q[j] - q[j + 2])
            back_a[1, j, here, :] = qu
            back_a[2, j, here, :] = qv
            back_a[3, j, here, :] = scale * (r[j] - r[j + 2])
            back_a[4, j, here, :] = ru
            back_a[5, j, here, :] = rv
            if 0 < i < tiles - 1:
                done = last[5, j, here, :] * q[j + 1] + last[2, j, here, :] * r[j + 1]
                done += prior[4, j, here, :] * qu + prior[5, j, here, :] * qv
                done += prior[1, j, here, :] * ru + prior[2, j, here, :] * rv
                curv[j, 8 * i - 8 : 8 * i, :] = -done
    turn(0, 5.0)
    turn(3, 5.0)
    send(0, state_hbm, 0).start()
    send(3, tangent_hbm, 0).start()

    def backward(k, carry):
        turn(1 + k)
        for i in range(tiles):
            step(back_a, back_b, i, -0.25, weigh(levels.at[ITERS - 3 - 2 * k]))
        send(1 + k, state_hbm, 1 + k).start()
        turn(4 + k)
        for i in range(tiles):
            step(back_b, back_a, i, -0.25, weigh(levels.at[ITERS - 4 - 2 * k]))
        send(4 + k, tangent_hbm, 1 + k).start()
        return carry

    lax.fori_loop(0, (ITERS - 2) // 2, backward, 0)
    for j in range(SLABS):
        nat[6, pl.ds(j + 1, 128, stride=SLABS), :] = curv[j].T
    curv_copy = pltpu.make_async_copy(nat.at[6, pl.ds(PAD, rows), :], curv_hbm, out_sem.at[6])
    curv_copy.start()
    for f in range(3):
        send(f, state_hbm, f).wait()
        send(3 + f, tangent_hbm, f).wait()
    curv_copy.wait()


def on_device(initial_state, bottom_drag, drag_direction, land_mask, section_cells, section_sign):
    rows, cols = bottom_drag.shape
    ext = cols + 2 * PAD
    f32, i32 = jnp.float32, jnp.int32
    hbm = pl.BlockSpec(memory_space=pl.ANY)
    lines = section_cells.shape[0] // 128
    tall = SLABS * 128 + 8
    vm, dma = pltpu.VMEM, pltpu.SemaphoreType.DMA
    fields = jax.ShapeDtypeStruct((5, SLABS, cols, 128), f32)
    halos = jax.ShapeDtypeStruct((2, 5, PAD, cols), f32)
    corners = jax.ShapeDtypeStruct((4, PAD, cols), f32)
    beside = jax.ShapeDtypeStruct((5, SLABS, PAD, 128), f32)
    weights = jax.ShapeDtypeStruct((SLABS, ext, 128), f32)
    given = pl.pallas_call(
        exchange_kernel,
        out_shape=(fields, halos, corners, beside, beside, weights),
        in_specs=[hbm] * 6,
        out_specs=(hbm,) * 6,
        scratch_shapes=[
            vm(fields.shape, f32),
            vm(weights.shape, f32),
            vm((3, rows, cols), f32),
            vm((rows, cols), f32),
            vm((rows, cols), f32),
            vm((rows, cols), i32),
            vm((lines, 128), i32),
            vm((lines, 128), i32),
            vm((5, tall, cols), f32),
            vm((5, PAD, cols), f32),
            vm((2, PAD, cols), f32),
            vm((4, lines, 128), i32),
            vm((2 * ext, LOW * 128), f32),
            vm((ext, 128), f32),
            dma((6,)),
            dma((8,)),
            dma((8,)),
            dma((8,)),
        ],
        compiler_params=pltpu.CompilerParams(
            collective_id=0, has_side_effects=True, vmem_limit_bytes=56 * 1024 * 1024
        ),
        name="exchange",
    )(
        initial_state, bottom_drag, drag_direction, land_mask,
        section_cells.reshape(lines, 128), section_sign.reshape(lines, 128),
    )
    return pl.pallas_call(
        chain_kernel,
        out_shape=(
            jax.ShapeDtypeStruct((rows, cols), f32),
            jax.ShapeDtypeStruct((3, rows, cols), f32),
            jax.ShapeDtypeStruct((3, rows, cols), f32),
        ),
        in_specs=[hbm] * 6,
        out_specs=(hbm, hbm, hbm),
        scratch_shapes=[
            vm((5, SLABS, ext, 128), f32),
            vm(halos.shape, f32),
            vm(corners.shape, f32),
            vm(beside.shape, f32),
            vm(beside.shape, f32),
            vm((3, 128, cols), f32),
            vm((cols, 128), f32),
            vm(weights.shape, f32),
            vm((ITERS, 6, SLABS, ext, 128), f32),
            vm((6, SLABS, ext, 128), f32),
            vm((6, SLABS, ext, 128), f32),
            vm((SLABS, ext, 128), f32),
            vm((SLABS, cols, 128), f32),
            vm((7, tall, cols), f32),
            dma((8,)),
            dma((7,)),
        ],
        compiler_params=pltpu.CompilerParams(vmem_limit_bytes=56 * 1024 * 1024),
        name="chain",
    )(*given)


def solution(mesh):
    return jax.shard_map(
        on_device,
        mesh=mesh,
        in_specs=(
            P(None, "lat", "lon"),
            P("lat", "lon"),
            P("lat", "lon"),
            P("lat", "lon"),
            P(),
            P(),
        ),
        out_specs=(P("lat", "lon"), P(None, "lat", "lon"), P(None, "lat", "lon")),
        check_vma=False,
    )
```

```python
import functools

import jax
import jax.numpy as jnp
from jax import lax
from jax.experimental import pallas as pl
from jax.experimental.pallas import tpu as pltpu
from jax.sharding import PartitionSpec as P

ITERS = 6
SLABS = 7
LOW = (SLABS + 1) // 2
PAD = 8
HALO_LANES = (17, 24, 49, 56, 81)
CHUNK = 8
MESH = pl.DeviceIdType.MESH


def patched(tile, halo_rows, at, j):
    lane = lax.broadcasted_iota(jnp.int32, tile.shape, 1)
    rolled = pltpu.roll(halo_rows, (128 - at - j) % 128, 1)
    north = 111 if j < 4 else 110
    here = lane == 0 if j == 4 else (lane == 0) | (lane == north)
    return jnp.where(here, rolled, tile)


def exchange_kernel(
    init_hbm, drag_hbm, dir_hbm, mask_hbm, cells_hbm, sign_hbm,
    t_hbm, halo, corner, from_west, from_east, w_hbm,
    t_ref, w_ref, init_ref, drag_ref, dir_ref, mask_ref, cells_ref, sign_ref,
    nat, north_tile, edge_tile, at_ref, acc, fold_acc, load_sem, send_sem, recv_sem, out_sem,
):
    rows, cols = drag_ref.shape
    ext = cols + 2 * PAD
    n_lon, n_lat = lax.axis_size("lon"), lax.axis_size("lat")
    lon, lat = lax.axis_index("lon"), lax.axis_index("lat")
    top = lat == n_lat - 1
    inner = lat > 0

    loads = [
        pltpu.make_async_copy(src, dst, load_sem.at[k])
        for k, (src, dst) in enumerate((
            (mask_hbm, mask_ref), (drag_hbm, drag_ref), (init_hbm, init_ref),
            (dir_hbm, dir_ref), (cells_hbm, cells_ref), (sign_hbm, sign_ref),
        ))
    ]
    def around(at, by):
        return lax.rem(at + by + n_lon, n_lon)

    up_lat = jnp.where(top, lat, lat + 1)
    up_lon = jnp.where(top, n_lon - 1 - lon, lon)
    up_half = jnp.where(top, 1, 0)
    turns = (0, 1, -1)
    ups = [around(up_lon, by) for by in turns]
    downs = [around(lon, by) for by in turns]
    own_fold = [top & (at == lon) for at in ups]

    def device(lon_at, lat_at):
        return {"lon": lon_at, "lat": lat_at}

    barrier = pltpu.get_barrier_semaphore()

    def greet(lon_at, lat_at):
        pl.semaphore_signal(
            barrier, inc=1, device_id=device(lon_at, lat_at), device_id_type=MESH
        )

    greet(around(lon, 1), lat)
    greet(around(lon, -1), lat)
    peers = 2
    for k in range(3):
        pl.when(jnp.logical_not(own_fold[k]))(functools.partial(greet, ups[k], up_lat))
        pl.when(inner)(functools.partial(greet, downs[k], lat - 1))
        peers += jnp.where(own_fold[k], 0, 1) + jnp.where(inner, 1, 0)
    for load in loads:
        load.start()

    def beside(fields):
        lane_of = lax.broadcasted_iota(jnp.int32, fields[0].shape, 1)
        sides = pltpu.roll(fields[0], 8, 1)
        for f in range(1, 5):
            sides = jnp.where(lane_of < 16 * f, sides, pltpu.roll(fields[f], 16 * f + 8, 1))
        return sides

    def prepare(part, carry):
        here = pl.ds(pl.multiple_of(part * 64, 64), 64)
        there = pl.ds(pl.multiple_of(part * 64 + PAD, 8), 64)
        ocean = mask_ref[here, :].astype(jnp.float32)
        inverse = 1.0 / (1.0 + drag_ref[here, :])
        fields = [
            init_ref[0, here, :] * (0.2 * ocean),
            init_ref[1, here, :] * ocean,
            init_ref[2, here, :] * ocean,
            ocean * inverse,
            -(dir_ref[here, :] * inverse),
        ]
        for f in range(5):
            nat[f, there, :] = fields[f]
        return carry

    height = nat.shape[1]
    tail = rows + PAD
    for f in range(5):
        nat[f, 0:PAD, :] = jnp.zeros((PAD, cols), jnp.float32)
        nat[f, tail:, :] = jnp.zeros((height - tail, cols), jnp.float32)
    for load in loads[:4]:
        load.wait()
    lax.fori_loop(0, rows // 64, prepare, 0)

    @pl.when(jnp.logical_not(top))
    def _():
        north_tile[...] = nat[:, rows : rows + PAD, :]

    @pl.when(top)
    def _():
        lanes = lax.broadcasted_iota(jnp.int32, (PAD, cols), 1)
        for f in range(5):
            tile = nat[f, rows : rows + PAD, :]
            turned = jnp.take_along_axis(tile, cols - 1 - lanes, axis=1)
            if f in (1, 2):
                turned = -turned
            for k in range(PAD):
                north_tile[f, k : k + 1, :] = turned[PAD - 1 - k : PAD - k, :]

    edge_tile[0] = beside([north_tile[f] for f in range(5)])
    edge_tile[1] = beside([nat[f, PAD : 2 * PAD, :] for f in range(5)])

    def fill(src, dst, which):
        return pltpu.make_async_copy(src, dst, out_sem.at[which])

    lowest = jnp.logical_not(inner)
    fills = [(lowest, fill(nat.at[:, pl.ds(tail, PAD), :], halo.at[0], 2))]
    for k in range(2):
        fills.append((lowest, fill(nat.at[0, pl.ds(tail, PAD), :], corner.at[k], 3 + k)))
        fills.append((own_fold[1 + k], fill(edge_tile.at[0], corner.at[2 + k], 5 + k)))
    for case, part in fills:
        pl.when(case)(part.start)

    def copy(src, dst, which, slot, lon_at, lat_at):
        return pltpu.make_async_remote_copy(
            src_ref=src, dst_ref=dst, send_sem=send_sem.at[which],
            recv_sem=recv_sem.at[slot], device_id=device(lon_at, lat_at),
            device_id_type=MESH,
        )

    up_copies = [copy(north_tile, halo.at[up_half], 0, up_half, ups[0], up_lat)]
    down_copies = [
        copy(nat.at[:, pl.ds(PAD, PAD), :], halo.at[1], 3, 1, downs[0], lat - 1)
    ]
    for k in range(2):
        slot = 2 * up_half + k
        up_copies.append(
            copy(edge_tile.at[0], corner.at[slot], 1 + k, 2 + slot, ups[1 + k], up_lat)
        )
        down_copies.append(
            copy(
                edge_tile.at[1], corner.at[2 + k], 4 + k, 4 + k,
                downs[1 + k], lat - 1,
            )
        )
    east_copy = copy(
        t_ref.at[:, :, pl.ds(cols - ITERS, ITERS), :],
        from_west.at[:, :, pl.ds(PAD - ITERS, ITERS), :], 6, 6, around(lon, 1), lat
    )
    west_copy = copy(
        t_ref.at[:, :, pl.ds(0, ITERS), :], from_east.at[:, :, pl.ds(0, ITERS), :], 7, 7, around(lon, -1), lat
    )

    for f in range(5):
        for j in range(SLABS):
            t_ref[f, j] = nat[f, pl.ds(j + 1, 128, stride=SLABS), :].T
    own_out = pltpu.make_async_copy(t_ref, t_hbm, out_sem.at[0])
    own_out.start()

    pl.semaphore_wait(barrier, peers)
    for k in (1, 2, 0):
        pl.when(jnp.logical_not(own_fold[k]))(up_copies[k].start)
        pl.when(inner)(down_copies[k].start)
    east_copy.start()
    west_copy.start()
    for load in loads[4:]:
        load.wait()

    total = cols * n_lon
    cell = cells_ref[...]
    row, col = lax.div(cell, total), lax.rem(cell, total)
    r = row - lat * rows + SLABS
    lane = lax.shift_right_arithmetic(r * 9363, 16)
    slab = r - lane * SLABS
    c = col - lon * cols + PAD
    c = jnp.where(c < 0, c + total, c)
    c = jnp.where(c >= total, c - total, c)
    in_rows = (r >= 0) & (r < rows + 2 * SLABS)
    at_ref[0] = jnp.where(c < ext, lax.div(slab, LOW) * ext + c, -1)
    at_ref[1] = jnp.where(in_rows, lax.rem(slab, LOW) * 128 + lane, -1)
    fr = rows - 1 - (row - lat * rows)
    at_ref[2] = jnp.where(top & (fr < SLABS), fr, -1)
    fc = total - 1 - col - lon * cols + PAD
    fc = jnp.where(fc < 0, fc + total, fc)
    at_ref[3] = jnp.where(fc >= total, fc - total, fc)

    contract = (((1,), (1,)), ((), ()))
    acc[...] = jnp.zeros_like(acc)
    fold_acc[...] = jnp.zeros_like(fold_acc)

    def spread(which, at):
        line = at_ref[which, pl.ds(at, 1), :]
        return jnp.broadcast_to(line, (16, 128)).astype(jnp.int16)

    def one_hot(which, first, size, value=None):
        steps = lax.broadcasted_iota(jnp.int16, (size, 128), 0)
        found = []
        for k in range(CHUNK):
            at = jnp.concatenate([spread(which, first + k)] * (size // 16), axis=0)
            if value is None:
                hit = jnp.ones((size, 128), jnp.bfloat16)
            else:
                hit = jnp.concatenate([value[k]] * (size // 16), axis=0)
            found.append(jnp.where(steps == at, hit, jnp.zeros((size, 128), jnp.bfloat16)))
        return jnp.concatenate(found, axis=1).astype(jnp.float8_e4m3fn)

    def signs_of(first):
        return [
            jnp.broadcast_to(sign_ref[pl.ds(first + k, 1), :], (16, 128))
            .astype(jnp.float32).astype(jnp.bfloat16)
            for k in range(CHUNK)
        ]

    def gather_weights(part, carry):
        first = part * CHUNK
        signs = signs_of(first)
        a = one_hot(0, first, 2 * ext)
        b = one_hot(1, first, LOW * 128, signs)
        acc[...] += lax.dot_general(a, b, contract, preferred_element_type=jnp.float32)
        return carry

    lax.fori_loop(0, cells_ref.shape[0] // CHUNK, gather_weights, 0)

    @pl.when(top)
    def _():
        def gather_ghosts(part, carry):
            first = part * CHUNK
            signs = signs_of(first)
            fa = one_hot(3, first, ext)
            fb = one_hot(2, first, 16, signs)
            fold_acc[:, 0:16] += lax.dot_general(
                fa, fb, contract, preferred_element_type=jnp.float32
            )
            return carry

        lax.fori_loop(0, cells_ref.shape[0] // CHUNK, gather_ghosts, 0)

    column = lax.broadcasted_iota(jnp.int32, (ext, 128), 1)
    ghosts = fold_acc[...]
    for j in range(SLABS):
        hi, lo = divmod(j, LOW)
        found = acc[hi * ext : (hi + 1) * ext, lo * 128 : (lo + 1) * 128]
        for k in range(SLABS):
            lane_at, slab_at = divmod(rows + SLABS + k, SLABS)
            if slab_at == j:
                turned = pltpu.roll(ghosts, lane_at - k, 1)
                found -= jnp.where(column == lane_at, turned, 0.0)
        w_ref[j] = found
    w_out = pltpu.make_async_copy(w_ref, w_hbm, out_sem.at[1])
    w_out.start()

    pl.when(inner)(copy(north_tile, halo.at[0], 0, 0, ups[0], up_lat).wait_recv)
    copy(north_tile, halo.at[1], 0, 1, ups[0], up_lat).wait_recv()
    for k in range(2):
        pl.when(inner)(
            copy(edge_tile.at[0], corner.at[k], 1 + k, 2 + k, ups[1 + k], up_lat).wait_recv
        )
        pl.when(jnp.logical_not(own_fold[1 + k]))(
            copy(edge_tile.at[0], corner.at[2 + k], 1 + k, 4 + k, ups[1 + k], up_lat).wait_recv
        )
    for case, part in fills:
        pl.when(case)(part.wait)
    for k in range(3):
        pl.when(jnp.logical_not(own_fold[k]))(up_copies[k].wait_send)
        pl.when(inner)(down_copies[k].wait_send)
    east_copy.wait_send()
    west_copy.wait_send()
    own_out.wait()
    w_out.wait()
    east_copy.wait_recv()
    west_copy.wait_recv()


def chain_kernel(
    t_hbm, halo_hbm, corner_hbm, west_hbm, east_hbm, w_hbm, curv_hbm, state_hbm, tangent_hbm,
    t_ref, halo, corner, from_west, from_east, pack, patch, w_ref, levels, back_a, back_b, scale_ref, curv, nat, load_sem, out_sem,
):
    ext = t_ref.shape[2]
    cols = ext - 2 * PAD
    rows = curv_hbm.shape[0]
    tiles = ext // 8
    bounds = (0, 16, 64, cols)
    sides = [
        pltpu.make_async_copy(src, dst, load_sem.at[k])
        for k, (src, dst) in enumerate((
            (halo_hbm, halo), (corner_hbm, corner), (west_hbm, from_west), (east_hbm, from_east)
        ))
    ]
    loads = [
        pltpu.make_async_copy(
            t_hbm.at[:, :, pl.ds(low, high - low), :],
            t_ref.at[:, :, pl.ds(PAD + low, high - low), :], load_sem.at[4 + k],
        )
        for k, (low, high) in enumerate(zip(bounds, bounds[1:]))
    ]
    w_load = pltpu.make_async_copy(w_hbm, w_ref, load_sem.at[7])
    for load in sides + loads + [w_load]:
        load.start()

    def around(src, field, j, i):
        if i == 0:
            low = pltpu.roll(src[field, j, 0:8, :], 1, 0)
        else:
            low = src[field, j, 8 * i - 1 : 8 * i + 7, :]
        if i == tiles - 1:
            high = pltpu.roll(src[field, j, 8 * i : 8 * i + 8, :], 7, 0)
        else:
            high = src[field, j, 8 * i + 1 : 8 * i + 9, :]
        return high - low

    def step(src, dst, i, spin, use=None, first=False):
        here = slice(8 * i, 8 * i + 8)
        parts = (0,) if first else (0, 3)

        def get(field, j):
            return src[field, j, here, :]

        up = {f: pltpu.roll(get(f, 0), 127, 1) for p in parts for f in (p, p + 2)}
        before = {f: pltpu.roll(get(f, SLABS - 1), 1, 1) for p in parts for f in (p, p + 2)}
        now = {f: get(f, 0) for p in parts for f in (p, p + 2)}
        for j in range(SLABS):
            damp, factor = t_ref[3, j, here, :], t_ref[4, j, here, :]
            if first:
                scale = jnp.where(damp > 0.0, 0.04, 0.0)
                scale_ref[j, here, :] = scale
            else:
                scale = scale_ref[j, here, :]
            after = {
                f: get(f, j + 1) if j < SLABS - 1 else up[f] for p in parts for f in (p, p + 2)
            }
            new = []
            for p in parts:
                h, u, v = p, p + 1, p + 2
                um, vm = get(u, j), now[v]
                new_h = now[h] - scale * (around(src, u, j, i) + (after[v] - before[v]))
                new_u = (um - around(src, h, j, i) + spin * vm) * damp
                new_v = (vm - (after[h] - before[h]) - spin * um) * damp
                if p:
                    new_u += factor * new[0]
                    new_v += factor * new[1]
                new += [new_u, new_v]
                dst[h, j, here, :] = new_h
                dst[u, j, here, :] = new_u
                dst[v, j, here, :] = new_v
            if first:
                new += [factor * new[0], factor * new[1]]
                dst[3, j, here, :] = jnp.zeros((8, 128), jnp.float32)
                dst[4, j, here, :] = new[2]
                dst[5, j, here, :] = new[3]
            if use is not None:
                use(j, i, here, new)
            before, now = now, after

    def weigh(level):
        def use(j, i, here, new):
            if 0 < i < tiles - 1:
                qu, qv, ru, rv = new
                own = slice(8 * i - 8, 8 * i)
                curv[j, own, :] -= (
                    level[4, j, here, :] * qu + level[5, j, here, :] * qv
                ) + (level[1, j, here, :] * ru + level[2, j, here, :] * rv)
        return use

    def turn(field, times=None):
        for j in range(SLABS):
            block = levels[ITERS - 1, field, j, PAD : PAD + cols, :]
            if times is not None:
                block = block * times
            nat[field, pl.ds(j + 1, 128, stride=SLABS), :] = block.T

    def send(field, out, at):
        return pltpu.make_async_copy(
            nat.at[field, pl.ds(PAD, rows), :], out.at[at], out_sem.at[field]
        )

    pack[...] = jnp.zeros_like(pack)
    sides[0].wait()
    sides[1].wait()

    def place_rows(k, at, south, north):
        pack[k, at : at + 7, :] = south[1:8]
        pack[k, at - 17 : at - 13, :] = north[2:6]
        pack[k, at - 13 : at - 11, :] = north[0:2]

    for f in range(5):
        place_rows(0, HALO_LANES[f], halo[0, f], halo[1, f])
    for k in range(2):
        place_rows(1 + k, HALO_LANES[0], corner[k], corner[2 + k])
    patch[...] = pack[0].T
    corners = pack[1].T, pack[2].T
    sides[2].wait()
    sides[3].wait()
    line = lax.broadcasted_iota(jnp.int32, (PAD, 128), 0)
    sent = line >= PAD - ITERS, line < ITERS
    for k, (got, place) in enumerate(((from_west, 0), (from_east, cols + PAD))):
        for f in range(5):
            rows_in = corners[k][16 * f + 8 * k : 16 * f + 8 * k + 8]
            for j in range(SLABS):
                tile = jnp.where(sent[k], got[f, j], 0.0)
                t_ref[f, j, place : place + PAD, :] = patched(
                    tile, rows_in, HALO_LANES[0], j
                )

    for i in range(tiles):
        for load, low in zip(loads, bounds):
            if 8 * i == low:
                load.wait()
        if i < tiles - 2:
            here = slice(8 * i + PAD, 8 * i + PAD + 8)
            halo_rows = patch[8 * i : 8 * i + 8, :]
            for f in range(5):
                for j in range(SLABS):
                    t_ref[f, j, here, :] = patched(
                        t_ref[f, j, here, :], halo_rows, HALO_LANES[f], j
                    )
        step(t_ref, levels.at[0], i, 0.25, first=True)

    def forward(n, carry):
        for i in range(tiles):
            step(levels.at[n], levels.at[n + 1], i, 0.25)
        return carry

    lax.fori_loop(0, ITERS - 1, forward, 0)

    w_load.wait()
    last, prior = levels.at[ITERS - 1], levels.at[ITERS - 2]
    for i in range(tiles):
        here = slice(8 * i, 8 * i + 8)
        q = [t_ref[3, j, here, :] * w_ref[j, here, :] for j in range(SLABS)]
        r = [t_ref[4, j, here, :] * q[j] for j in range(SLABS)]
        q = [pltpu.roll(q[-1], 1, 1)] + q + [pltpu.roll(q[0], 127, 1)]
        r = [pltpu.roll(r[-1], 1, 1)] + r + [pltpu.roll(r[0], 127, 1)]
        for j in range(SLABS):
            damp, factor = t_ref[3, j, here, :], t_ref[4, j, here, :]
            scale = scale_ref[j, here, :]
            qv, rv = q[j + 1] * damp, r[j + 1] * damp
            qu, ru = -0.25 * qv, -0.25 * rv
            rv, ru = rv + factor * qv, ru + factor * qu
            back_a[0, j, here, :] = scale * (q[j] - q[j + 2])
            back_a[1, j, here, :] = qu
            back_a[2, j, here, :] = qv
            back_a[3, j, here, :] = scale * (r[j] - r[j + 2])
            back_a[4, j, here, :] = ru
            back_a[5, j, here, :] = rv
            if 0 < i < tiles - 1:
                done = last[5, j, here, :] * q[j + 1] + last[2, j, here, :] * r[j + 1]
                done += prior[4, j, here, :] * qu + prior[5, j, here, :] * qv
                done += prior[1, j, here, :] * ru + prior[2, j, here, :] * rv
                curv[j, 8 * i - 8 : 8 * i, :] = -done
    turn(0, 5.0)
    turn(3, 5.0)
    send(0, state_hbm, 0).start()
    send(3, tangent_hbm, 0).start()

    def backward(k, carry):
        turn(1 + k)
        for i in range(tiles):
            step(back_a, back_b, i, -0.25, weigh(levels.at[ITERS - 3 - 2 * k]))
        send(1 + k, state_hbm, 1 + k).start()
        turn(4 + k)
        for i in range(tiles):
            step(back_b, back_a, i, -0.25, weigh(levels.at[ITERS - 4 - 2 * k]))
        send(4 + k, tangent_hbm, 1 + k).start()
        return carry

    lax.fori_loop(0, (ITERS - 2) // 2, backward, 0)
    for j in range(SLABS):
        nat[6, pl.ds(j + 1, 128, stride=SLABS), :] = curv[j].T
    curv_copy = pltpu.make_async_copy(nat.at[6, pl.ds(PAD, rows), :], curv_hbm, out_sem.at[6])
    curv_copy.start()
    for f in range(3):
        send(f, state_hbm, f).wait()
        send(3 + f, tangent_hbm, f).wait()
    curv_copy.wait()


def on_device(initial_state, bottom_drag, drag_direction, land_mask, section_cells, section_sign):
    rows, cols = bottom_drag.shape
    ext = cols + 2 * PAD
    f32, i32 = jnp.float32, jnp.int32
    hbm = pl.BlockSpec(memory_space=pl.ANY)
    lines = section_cells.shape[0] // 128
    tall = SLABS * 128 + 8
    vm, dma = pltpu.VMEM, pltpu.SemaphoreType.DMA
    fields = jax.ShapeDtypeStruct((5, SLABS, cols, 128), f32)
    halos = jax.ShapeDtypeStruct((2, 5, PAD, cols), f32)
    corners = jax.ShapeDtypeStruct((4, PAD, cols), f32)
    beside = jax.ShapeDtypeStruct((5, SLABS, PAD, 128), f32)
    weights = jax.ShapeDtypeStruct((SLABS, ext, 128), f32)
    given = pl.pallas_call(
        exchange_kernel,
        out_shape=(fields, halos, corners, beside, beside, weights),
        in_specs=[hbm] * 6,
        out_specs=(hbm,) * 6,
        scratch_shapes=[
            vm(fields.shape, f32),
            vm(weights.shape, f32),
            vm((3, rows, cols), f32),
            vm((rows, cols), f32),
            vm((rows, cols), f32),
            vm((rows, cols), i32),
            vm((lines, 128), i32),
            vm((lines, 128), i32),
            vm((5, tall, cols), f32),
            vm((5, PAD, cols), f32),
            vm((2, PAD, cols), f32),
            vm((4, lines, 128), i32),
            vm((2 * ext, LOW * 128), f32),
            vm((ext, 128), f32),
            dma((6,)),
            dma((8,)),
            dma((8,)),
            dma((8,)),
        ],
        compiler_params=pltpu.CompilerParams(
            collective_id=0, has_side_effects=True, vmem_limit_bytes=56 * 1024 * 1024
        ),
        name="exchange",
    )(
        initial_state, bottom_drag, drag_direction, land_mask,
        section_cells.reshape(lines, 128), section_sign.reshape(lines, 128),
    )
    return pl.pallas_call(
        chain_kernel,
        out_shape=(
            jax.ShapeDtypeStruct((rows, cols), f32),
            jax.ShapeDtypeStruct((3, rows, cols), f32),
            jax.ShapeDtypeStruct((3, rows, cols), f32),
        ),
        in_specs=[hbm] * 6,
        out_specs=(hbm, hbm, hbm),
        scratch_shapes=[
            vm((5, SLABS, ext, 128), f32),
            vm(halos.shape, f32),
            vm(corners.shape, f32),
            vm(beside.shape, f32),
            vm(beside.shape, f32),
            vm((3, 128, cols), f32),
            vm((cols, 128), f32),
            vm(weights.shape, f32),
            vm((ITERS, 6, SLABS, ext, 128), f32),
            vm((6, SLABS, ext, 128), f32),
            vm((6, SLABS, ext, 128), f32),
            vm((SLABS, ext, 128), f32),
            vm((SLABS, cols, 128), f32),
            vm((7, tall, cols), f32),
            dma((8,)),
            dma((7,)),
        ],
        compiler_params=pltpu.CompilerParams(vmem_limit_bytes=56 * 1024 * 1024),
        name="chain",
    )(*given)


def solution(mesh):
    return jax.shard_map(
        on_device,
        mesh=mesh,
        in_specs=(
            P(None, "lat", "lon"),
            P("lat", "lon"),
            P("lat", "lon"),
            P("lat", "lon"),
            P(),
            P(),
        ),
        out_specs=(P("lat", "lon"), P(None, "lat", "lon"), P(None, "lat", "lon")),
        check_vma=False,
    )
```

```python
import functools

import jax
import jax.numpy as jnp
from jax import lax
from jax.experimental import pallas as pl
from jax.experimental.pallas import tpu as pltpu
from jax.sharding import PartitionSpec as P

ITERS = 6
SLABS = 7
LOW = (SLABS + 1) // 2
PAD = 8
HALO_LANES = (17, 24, 49, 56, 81)
CHUNK = 8
MESH = pl.DeviceIdType.MESH


def patched(tile, halo_rows, at, j):
    lane = lax.broadcasted_iota(jnp.int32, tile.shape, 1)
    rolled = pltpu.roll(halo_rows, (128 - at - j) % 128, 1)
    north = 111 if j < 4 else 110
    here = lane == 0 if j == 4 else (lane == 0) | (lane == north)
    return jnp.where(here, rolled, tile)


def exchange_kernel(
    init_hbm, drag_hbm, dir_hbm, mask_hbm, cells_hbm, sign_hbm,
    t_hbm, halo, corner, from_west, from_east, w_hbm,
    t_ref, w_ref, init_ref, drag_ref, dir_ref, mask_ref, cells_ref, sign_ref,
    nat, north_tile, edge_tile, at_ref, acc, fold_acc, load_sem, send_sem, recv_sem, out_sem,
):
    rows, cols = drag_ref.shape
    ext = cols + 2 * PAD
    n_lon, n_lat = lax.axis_size("lon"), lax.axis_size("lat")
    lon, lat = lax.axis_index("lon"), lax.axis_index("lat")
    top = lat == n_lat - 1
    inner = lat > 0

    loads = [
        pltpu.make_async_copy(src, dst, load_sem.at[k])
        for k, (src, dst) in enumerate((
            (mask_hbm, mask_ref), (drag_hbm, drag_ref), (init_hbm, init_ref),
            (dir_hbm, dir_ref), (cells_hbm, cells_ref), (sign_hbm, sign_ref),
        ))
    ]
    def around(at, by):
        return lax.rem(at + by + n_lon, n_lon)

    up_lat = jnp.where(top, lat, lat + 1)
    up_lon = jnp.where(top, n_lon - 1 - lon, lon)
    up_half = jnp.where(top, 1, 0)
    turns = (0, 1, -1)
    ups = [around(up_lon, by) for by in turns]
    downs = [around(lon, by) for by in turns]
    own_fold = [top & (at == lon) for at in ups]

    def device(lon_at, lat_at):
        return {"lon": lon_at, "lat": lat_at}

    barrier = pltpu.get_barrier_semaphore()

    def greet(lon_at, lat_at):
        pl.semaphore_signal(
            barrier, inc=1, device_id=device(lon_at, lat_at), device_id_type=MESH
        )

    greet(around(lon, 1), lat)
    greet(around(lon, -1), lat)
    peers = 2
    for k in range(3):
        pl.when(jnp.logical_not(own_fold[k]))(functools.partial(greet, ups[k], up_lat))
        pl.when(inner)(functools.partial(greet, downs[k], lat - 1))
        peers += jnp.where(own_fold[k], 0, 1) + jnp.where(inner, 1, 0)
    for load in loads:
        load.start()

    def beside(fields):
        lane_of = lax.broadcasted_iota(jnp.int32, fields[0].shape, 1)
        sides = pltpu.roll(fields[0], 8, 1)
        for f in range(1, 5):
            sides = jnp.where(lane_of < 16 * f, sides, pltpu.roll(fields[f], 16 * f + 8, 1))
        return sides

    def prepare(part, carry):
        here = pl.ds(pl.multiple_of(part * 64, 64), 64)
        there = pl.ds(pl.multiple_of(part * 64 + PAD, 8), 64)
        ocean = mask_ref[here, :].astype(jnp.float32)
        inverse = 1.0 / (1.0 + drag_ref[here, :])
        fields = [
            init_ref[0, here, :] * (0.2 * ocean),
            init_ref[1, here, :] * ocean,
            init_ref[2, here, :] * ocean,
            ocean * inverse,
            -(dir_ref[here, :] * inverse),
        ]
        for f in range(5):
            nat[f, there, :] = fields[f]
        return carry

    height = nat.shape[1]
    tail = rows + PAD
    for f in range(5):
        nat[f, 0:PAD, :] = jnp.zeros((PAD, cols), jnp.float32)
        nat[f, tail:, :] = jnp.zeros((height - tail, cols), jnp.float32)
    for load in loads[:4]:
        load.wait()
    lax.fori_loop(0, rows // 64, prepare, 0)

    @pl.when(jnp.logical_not(top))
    def _():
        north_tile[...] = nat[:, rows : rows + PAD, :]

    @pl.when(top)
    def _():
        lanes = lax.broadcasted_iota(jnp.int32, (PAD, cols), 1)
        for f in range(5):
            tile = nat[f, rows : rows + PAD, :]
            turned = jnp.take_along_axis(tile, cols - 1 - lanes, axis=1)
            if f in (1, 2):
                turned = -turned
            for k in range(PAD):
                north_tile[f, k : k + 1, :] = turned[PAD - 1 - k : PAD - k, :]

    edge_tile[0] = beside([north_tile[f] for f in range(5)])
    edge_tile[1] = beside([nat[f, PAD : 2 * PAD, :] for f in range(5)])

    def fill(src, dst, which):
        return pltpu.make_async_copy(src, dst, out_sem.at[which])

    lowest = jnp.logical_not(inner)
    fills = [(lowest, fill(nat.at[:, pl.ds(tail, PAD), :], halo.at[0], 2))]
    for k in range(2):
        fills.append((lowest, fill(nat.at[0, pl.ds(tail, PAD), :], corner.at[k], 3 + k)))
        fills.append((own_fold[1 + k], fill(edge_tile.at[0], corner.at[2 + k], 5 + k)))
    for case, part in fills:
        pl.when(case)(part.start)

    def copy(src, dst, which, slot, lon_at, lat_at):
        return pltpu.make_async_remote_copy(
            src_ref=src, dst_ref=dst, send_sem=send_sem.at[which],
            recv_sem=recv_sem.at[slot], device_id=device(lon_at, lat_at),
            device_id_type=MESH,
        )

    up_copies = [copy(north_tile, halo.at[up_half], 0, up_half, ups[0], up_lat)]
    down_copies = [
        copy(nat.at[:, pl.ds(PAD, PAD), :], halo.at[1], 3, 1, downs[0], lat - 1)
    ]
    for k in range(2):
        slot = 2 * up_half + k
        up_copies.append(
            copy(edge_tile.at[0], corner.at[slot], 1 + k, 2 + slot, ups[1 + k], up_lat)
        )
        down_copies.append(
            copy(
                edge_tile.at[1], corner.at[2 + k], 4 + k, 4 + k,
                downs[1 + k], lat - 1,
            )
        )
    east_copy = copy(
        t_ref.at[:, :, pl.ds(cols - ITERS, ITERS), :],
        from_west.at[:, :, pl.ds(PAD - ITERS, ITERS), :], 6, 6, around(lon, 1), lat
    )
    west_copy = copy(
        t_ref.at[:, :, pl.ds(0, ITERS), :], from_east.at[:, :, pl.ds(0, ITERS), :], 7, 7, around(lon, -1), lat
    )

    for f in range(5):
        for j in range(SLABS):
            t_ref[f, j] = nat[f, pl.ds(j + 1, 128, stride=SLABS), :].T
    own_out = pltpu.make_async_copy(t_ref, t_hbm, out_sem.at[0])
    own_out.start()

    pl.semaphore_wait(barrier, peers)
    for k in (1, 2, 0):
        pl.when(jnp.logical_not(own_fold[k]))(up_copies[k].start)
        pl.when(inner)(down_copies[k].start)
    east_copy.start()
    west_copy.start()
    for load in loads[4:]:
        load.wait()

    total = cols * n_lon
    cell = cells_ref[...]
    row, col = lax.div(cell, total), lax.rem(cell, total)
    r = row - lat * rows + SLABS
    lane = lax.shift_right_arithmetic(r * 9363, 16)
    slab = r - lane * SLABS
    c = col - lon * cols + PAD
    c = jnp.where(c < 0, c + total, c)
    c = jnp.where(c >= total, c - total, c)
    in_rows = (r >= 0) & (r < rows + 2 * SLABS)
    at_ref[0] = jnp.where(c < ext, lax.div(slab, LOW) * ext + c, -1)
    at_ref[1] = jnp.where(in_rows, lax.rem(slab, LOW) * 128 + lane, -1)
    fr = rows - 1 - (row - lat * rows)
    at_ref[2] = jnp.where(top & (fr < SLABS), fr, -1)
    fc = total - 1 - col - lon * cols + PAD
    fc = jnp.where(fc < 0, fc + total, fc)
    at_ref[3] = jnp.where(fc >= total, fc - total, fc)

    contract = (((1,), (1,)), ((), ()))
    acc[...] = jnp.zeros_like(acc)
    fold_acc[...] = jnp.zeros_like(fold_acc)

    def spread(which, at):
        line = at_ref[which, pl.ds(at, 1), :]
        return jnp.broadcast_to(line, (16, 128)).astype(jnp.int16)

    def one_hot(which, first, size, value=None):
        steps = lax.broadcasted_iota(jnp.int16, (size, 128), 0)
        found = []
        for k in range(CHUNK):
            at = jnp.concatenate([spread(which, first + k)] * (size // 16), axis=0)
            if value is None:
                hit = jnp.ones((size, 128), jnp.bfloat16)
            else:
                hit = jnp.concatenate([value[k]] * (size // 16), axis=0)
            found.append(jnp.where(steps == at, hit, jnp.zeros((size, 128), jnp.bfloat16)))
        return jnp.concatenate(found, axis=1).astype(jnp.float8_e4m3fn)

    def signs_of(first):
        return [
            jnp.broadcast_to(sign_ref[pl.ds(first + k, 1), :], (16, 128))
            .astype(jnp.float32).astype(jnp.bfloat16)
            for k in range(CHUNK)
        ]

    def gather_weights(part, carry):
        first = part * CHUNK
        signs = signs_of(first)
        a = one_hot(0, first, 2 * ext)
        b = one_hot(1, first, LOW * 128, signs)
        acc[...] += lax.dot_general(a, b, contract, preferred_element_type=jnp.float32)
        return carry

    lax.fori_loop(0, cells_ref.shape[0] // CHUNK, gather_weights, 0)

    @pl.when(top)
    def _():
        def gather_ghosts(part, carry):
            first = part * CHUNK
            signs = signs_of(first)
            fa = one_hot(3, first, ext)
            fb = one_hot(2, first, 16, signs)
            fold_acc[:, 0:16] += lax.dot_general(
                fa, fb, contract, preferred_element_type=jnp.float32
            )
            return carry

        lax.fori_loop(0, cells_ref.shape[0] // CHUNK, gather_ghosts, 0)

    column = lax.broadcasted_iota(jnp.int32, (ext, 128), 1)
    ghosts = fold_acc[...]
    w_outs = []
    for j in range(SLABS):
        hi, lo = divmod(j, LOW)
        found = acc[hi * ext : (hi + 1) * ext, lo * 128 : (lo + 1) * 128]
        for k in range(SLABS):
            lane_at, slab_at = divmod(rows + SLABS + k, SLABS)
            if slab_at == j:
                turned = pltpu.roll(ghosts, lane_at - k, 1)
                found -= jnp.where(column == lane_at, turned, 0.0)
        w_ref[j] = found
        w_outs.append(pltpu.make_async_copy(w_ref.at[j], w_hbm.at[j], out_sem.at[7 + j]))
        w_outs[j].start()

    pl.when(inner)(copy(north_tile, halo.at[0], 0, 0, ups[0], up_lat).wait_recv)
    copy(north_tile, halo.at[1], 0, 1, ups[0], up_lat).wait_recv()
    for k in range(2):
        pl.when(inner)(
            copy(edge_tile.at[0], corner.at[k], 1 + k, 2 + k, ups[1 + k], up_lat).wait_recv
        )
        pl.when(jnp.logical_not(own_fold[1 + k]))(
            copy(edge_tile.at[0], corner.at[2 + k], 1 + k, 4 + k, ups[1 + k], up_lat).wait_recv
        )
    for case, part in fills:
        pl.when(case)(part.wait)
    for k in range(3):
        pl.when(jnp.logical_not(own_fold[k]))(up_copies[k].wait_send)
        pl.when(inner)(down_copies[k].wait_send)
    east_copy.wait_send()
    west_copy.wait_send()
    own_out.wait()
    for w_out in w_outs:
        w_out.wait()
    east_copy.wait_recv()
    west_copy.wait_recv()


def chain_kernel(
    t_hbm, halo_hbm, corner_hbm, west_hbm, east_hbm, w_hbm, curv_hbm, state_hbm, tangent_hbm,
    t_ref, halo, corner, from_west, from_east, pack, patch, w_ref, levels, back_a, back_b, scale_ref, curv, nat, load_sem, out_sem,
):
    ext = t_ref.shape[2]
    cols = ext - 2 * PAD
    rows = curv_hbm.shape[0]
    tiles = ext // 8
    bounds = (0, 16, 64, cols)
    sides = [
        pltpu.make_async_copy(src, dst, load_sem.at[k])
        for k, (src, dst) in enumerate((
            (halo_hbm, halo), (corner_hbm, corner), (west_hbm, from_west), (east_hbm, from_east)
        ))
    ]
    loads = [
        pltpu.make_async_copy(
            t_hbm.at[:, :, pl.ds(low, high - low), :],
            t_ref.at[:, :, pl.ds(PAD + low, high - low), :], load_sem.at[4 + k],
        )
        for k, (low, high) in enumerate(zip(bounds, bounds[1:]))
    ]
    w_load = pltpu.make_async_copy(w_hbm, w_ref, load_sem.at[7])
    for load in sides + loads + [w_load]:
        load.start()

    def around(src, field, j, i):
        if i == 0:
            low = pltpu.roll(src[field, j, 0:8, :], 1, 0)
        else:
            low = src[field, j, 8 * i - 1 : 8 * i + 7, :]
        if i == tiles - 1:
            high = pltpu.roll(src[field, j, 8 * i : 8 * i + 8, :], 7, 0)
        else:
            high = src[field, j, 8 * i + 1 : 8 * i + 9, :]
        return high - low

    def step(src, dst, i, spin, use=None, first=False):
        here = slice(8 * i, 8 * i + 8)
        parts = (0,) if first else (0, 3)

        def get(field, j):
            return src[field, j, here, :]

        up = {f: pltpu.roll(get(f, 0), 127, 1) for p in parts for f in (p, p + 2)}
        before = {f: pltpu.roll(get(f, SLABS - 1), 1, 1) for p in parts for f in (p, p + 2)}
        now = {f: get(f, 0) for p in parts for f in (p, p + 2)}
        for j in range(SLABS):
            damp, factor = t_ref[3, j, here, :], t_ref[4, j, here, :]
            if first:
                scale = jnp.where(damp > 0.0, 0.04, 0.0)
                scale_ref[j, here, :] = scale
            else:
                scale = scale_ref[j, here, :]
            after = {
                f: get(f, j + 1) if j < SLABS - 1 else up[f] for p in parts for f in (p, p + 2)
            }
            new = []
            for p in parts:
                h, u, v = p, p + 1, p + 2
                um, vm = get(u, j), now[v]
                new_h = now[h] - scale * (around(src, u, j, i) + (after[v] - before[v]))
                new_u = (um - around(src, h, j, i) + spin * vm) * damp
                new_v = (vm - (after[h] - before[h]) - spin * um) * damp
                if p:
                    new_u += factor * new[0]
                    new_v += factor * new[1]
                new += [new_u, new_v]
                dst[h, j, here, :] = new_h
                dst[u, j, here, :] = new_u
                dst[v, j, here, :] = new_v
            if first:
                new += [factor * new[0], factor * new[1]]
                dst[3, j, here, :] = jnp.zeros((8, 128), jnp.float32)
                dst[4, j, here, :] = new[2]
                dst[5, j, here, :] = new[3]
            if use is not None:
                use(j, i, here, new)
            before, now = now, after

    def weigh(level):
        def use(j, i, here, new):
            if 0 < i < tiles - 1:
                qu, qv, ru, rv = new
                own = slice(8 * i - 8, 8 * i)
                curv[j, own, :] -= (
                    level[4, j, here, :] * qu + level[5, j, here, :] * qv
                ) + (level[1, j, here, :] * ru + level[2, j, here, :] * rv)
        return use

    def turn(field, times=None):
        for j in range(SLABS):
            block = levels[ITERS - 1, field, j, PAD : PAD + cols, :]
            if times is not None:
                block = block * times
            nat[field, pl.ds(j + 1, 128, stride=SLABS), :] = block.T

    def send(field, out, at):
        return pltpu.make_async_copy(
            nat.at[field, pl.ds(PAD, rows), :], out.at[at], out_sem.at[field]
        )

    pack[...] = jnp.zeros_like(pack)
    sides[0].wait()
    sides[1].wait()

    def place_rows(k, at, south, north):
        pack[k, at : at + 7, :] = south[1:8]
        pack[k, at - 17 : at - 13, :] = north[2:6]
        pack[k, at - 13 : at - 11, :] = north[0:2]

    for f in range(5):
        place_rows(0, HALO_LANES[f], halo[0, f], halo[1, f])
    for k in range(2):
        place_rows(1 + k, HALO_LANES[0], corner[k], corner[2 + k])
    patch[...] = pack[0].T
    corners = pack[1].T, pack[2].T
    sides[2].wait()
    sides[3].wait()
    line = lax.broadcasted_iota(jnp.int32, (PAD, 128), 0)
    sent = line >= PAD - ITERS, line < ITERS
    for k, (got, place) in enumerate(((from_west, 0), (from_east, cols + PAD))):
        for f in range(5):
            rows_in = corners[k][16 * f + 8 * k : 16 * f + 8 * k + 8]
            for j in range(SLABS):
                tile = jnp.where(sent[k], got[f, j], 0.0)
                t_ref[f, j, place : place + PAD, :] = patched(
                    tile, rows_in, HALO_LANES[0], j
                )

    for i in range(tiles):
        for load, low in zip(loads, bounds):
            if 8 * i == low:
                load.wait()
        if i < tiles - 2:
            here = slice(8 * i + PAD, 8 * i + PAD + 8)
            halo_rows = patch[8 * i : 8 * i + 8, :]
            for f in range(5):
                for j in range(SLABS):
                    t_ref[f, j, here, :] = patched(
                        t_ref[f, j, here, :], halo_rows, HALO_LANES[f], j
                    )
        step(t_ref, levels.at[0], i, 0.25, first=True)

    def forward(n, carry):
        for i in range(tiles):
            step(levels.at[n], levels.at[n + 1], i, 0.25)
        return carry

    lax.fori_loop(0, ITERS - 1, forward, 0)

    w_load.wait()
    last, prior = levels.at[ITERS - 1], levels.at[ITERS - 2]
    for i in range(tiles):
        here = slice(8 * i, 8 * i + 8)
        q = [t_ref[3, j, here, :] * w_ref[j, here, :] for j in range(SLABS)]
        r = [t_ref[4, j, here, :] * q[j] for j in range(SLABS)]
        q = [pltpu.roll(q[-1], 1, 1)] + q + [pltpu.roll(q[0], 127, 1)]
        r = [pltpu.roll(r[-1], 1, 1)] + r + [pltpu.roll(r[0], 127, 1)]
        for j in range(SLABS):
            damp, factor = t_ref[3, j, here, :], t_ref[4, j, here, :]
            scale = scale_ref[j, here, :]
            qv, rv = q[j + 1] * damp, r[j + 1] * damp
            qu, ru = -0.25 * qv, -0.25 * rv
            rv, ru = rv + factor * qv, ru + factor * qu
            back_a[0, j, here, :] = scale * (q[j] - q[j + 2])
            back_a[1, j, here, :] = qu
            back_a[2, j, here, :] = qv
            back_a[3, j, here, :] = scale * (r[j] - r[j + 2])
            back_a[4, j, here, :] = ru
            back_a[5, j, here, :] = rv
            if 0 < i < tiles - 1:
                done = last[5, j, here, :] * q[j + 1] + last[2, j, here, :] * r[j + 1]
                done += prior[4, j, here, :] * qu + prior[5, j, here, :] * qv
                done += prior[1, j, here, :] * ru + prior[2, j, here, :] * rv
                curv[j, 8 * i - 8 : 8 * i, :] = -done
    turn(0, 5.0)
    turn(3, 5.0)
    send(0, state_hbm, 0).start()
    send(3, tangent_hbm, 0).start()

    def backward(k, carry):
        turn(1 + k)
        for i in range(tiles):
            step(back_a, back_b, i, -0.25, weigh(levels.at[ITERS - 3 - 2 * k]))
        send(1 + k, state_hbm, 1 + k).start()
        turn(4 + k)
        for i in range(tiles):
            step(back_b, back_a, i, -0.25, weigh(levels.at[ITERS - 4 - 2 * k]))
        send(4 + k, tangent_hbm, 1 + k).start()
        return carry

    lax.fori_loop(0, (ITERS - 2) // 2, backward, 0)
    for j in range(SLABS):
        nat[6, pl.ds(j + 1, 128, stride=SLABS), :] = curv[j].T
    curv_copy = pltpu.make_async_copy(nat.at[6, pl.ds(PAD, rows), :], curv_hbm, out_sem.at[6])
    curv_copy.start()
    for f in range(3):
        send(f, state_hbm, f).wait()
        send(3 + f, tangent_hbm, f).wait()
    curv_copy.wait()


def on_device(initial_state, bottom_drag, drag_direction, land_mask, section_cells, section_sign):
    rows, cols = bottom_drag.shape
    ext = cols + 2 * PAD
    f32, i32 = jnp.float32, jnp.int32
    hbm = pl.BlockSpec(memory_space=pl.ANY)
    lines = section_cells.shape[0] // 128
    tall = SLABS * 128 + 8
    vm, dma = pltpu.VMEM, pltpu.SemaphoreType.DMA
    fields = jax.ShapeDtypeStruct((5, SLABS, cols, 128), f32)
    halos = jax.ShapeDtypeStruct((2, 5, PAD, cols), f32)
    corners = jax.ShapeDtypeStruct((4, PAD, cols), f32)
    beside = jax.ShapeDtypeStruct((5, SLABS, PAD, 128), f32)
    weights = jax.ShapeDtypeStruct((SLABS, ext, 128), f32)
    given = pl.pallas_call(
        exchange_kernel,
        out_shape=(fields, halos, corners, beside, beside, weights),
        in_specs=[hbm] * 6,
        out_specs=(hbm,) * 6,
        scratch_shapes=[
            vm(fields.shape, f32),
            vm(weights.shape, f32),
            vm((3, rows, cols), f32),
            vm((rows, cols), f32),
            vm((rows, cols), f32),
            vm((rows, cols), i32),
            vm((lines, 128), i32),
            vm((lines, 128), i32),
            vm((5, tall, cols), f32),
            vm((5, PAD, cols), f32),
            vm((2, PAD, cols), f32),
            vm((4, lines, 128), i32),
            vm((2 * ext, LOW * 128), f32),
            vm((ext, 128), f32),
            dma((6,)),
            dma((8,)),
            dma((8,)),
            dma((7 + SLABS,)),
        ],
        compiler_params=pltpu.CompilerParams(
            collective_id=0, has_side_effects=True, vmem_limit_bytes=56 * 1024 * 1024
        ),
        name="exchange",
    )(
        initial_state, bottom_drag, drag_direction, land_mask,
        section_cells.reshape(lines, 128), section_sign.reshape(lines, 128),
    )
    return pl.pallas_call(
        chain_kernel,
        out_shape=(
            jax.ShapeDtypeStruct((rows, cols), f32),
            jax.ShapeDtypeStruct((3, rows, cols), f32),
            jax.ShapeDtypeStruct((3, rows, cols), f32),
        ),
        in_specs=[hbm] * 6,
        out_specs=(hbm, hbm, hbm),
        scratch_shapes=[
            vm((5, SLABS, ext, 128), f32),
            vm(halos.shape, f32),
            vm(corners.shape, f32),
            vm(beside.shape, f32),
            vm(beside.shape, f32),
            vm((3, 128, cols), f32),
            vm((cols, 128), f32),
            vm(weights.shape, f32),
            vm((ITERS, 6, SLABS, ext, 128), f32),
            vm((6, SLABS, ext, 128), f32),
            vm((6, SLABS, ext, 128), f32),
            vm((SLABS, ext, 128), f32),
            vm((SLABS, cols, 128), f32),
            vm((7, tall, cols), f32),
            dma((8,)),
            dma((7,)),
        ],
        compiler_params=pltpu.CompilerParams(vmem_limit_bytes=56 * 1024 * 1024),
        name="chain",
    )(*given)


def solution(mesh):
    return jax.shard_map(
        on_device,
        mesh=mesh,
        in_specs=(
            P(None, "lat", "lon"),
            P("lat", "lon"),
            P("lat", "lon"),
            P("lat", "lon"),
            P(),
            P(),
        ),
        out_specs=(P("lat", "lon"), P(None, "lat", "lon"), P(None, "lat", "lon")),
        check_vma=False,
    )
```
